512 devices in a mesh: group: 64 (over z_lo, y, core), tp: 8 (over x, z_hi).
Axes of the slice: x: 4, y: 8, z: 8 (z_hi: 2, z_lo: 4; z = z_hi * 4 + z_lo), core: 2. Of those that a mesh axis runs over, the one named last changes fastest.
Arguments:
- hidden: bfloat16 [3, 512, 5120], P(None, 'group'), may hold values from -6 to 6
- queries: bfloat16 [3, 512, 8192], P(None, 'group', 'tp'), as said below
- key_cache: bfloat16 [512, 512, 1024], P('group', None, 'tp'), as said below
- value_cache: bfloat16 [512, 512, 1024], P('group', None, 'tp'), may hold values from -6 to 6
- lengths: int32 [512], P('group'), may hold values from 1 to 512, 104857 in all
- key_gain: float32 [128], replicated, may hold values from 0.25 to 1.75
- base_weight: bfloat16 [5120, 2048], P(None, 'tp'), may hold values from -0.078125 to 0.078125
- delta_codes: bfloat16 [5120, 2048], P(('group', 'tp')), may hold values from -4 to 4
- delta_scales: bfloat16 [5120, 16], P(('group', 'tp')), may hold values from 0.0049743652 to 0.049804688
Outputs:
- attended: bfloat16 [3, 512, 8192], P(None, 'group', 'tp')
The draws below stay inside these ranges and needn't reach their ends.
Inputs may be any that keep to these rules, and one draw needn't show every extreme that they name: `queries`: query entries stay within -180 to 180. `key_cache`: cached key entries stay within -6 to 6. `lengths`: some row fills all 512 slots.
All inputs are finite; a program needn't handle non-finite values. No bound on the sum of `lengths` on one device may be relied on, other than what follows from the above.
Results may differ from the reference program's by a relative error of at most 0.0058.
Values may be sent and summed in bfloat16 or wider, within the bound.
A program may use at most 64 MiB of HBM per device.

```python
import math
import jax
import jax.numpy as jnp
import numpy as np
from jax import lax

D = 5120
HD = 128
KVH = 8
QH = 64
CAP = 512
STEPS = 3
ROWS = 512


def shared_keys(key):
    return jnp.clip(jax.random.normal(key, (ROWS, CAP, KVH * HD), jnp.float32), -6.0, 6.0)


def draw_key_cache(key, part):
    base = shared_keys(key)
    return base.astype(jnp.bfloat16)


def draw_queries(key, part):
    key = jax.random.fold_in(key, 12)
    noise = jnp.clip(jax.random.normal(key, (STEPS, ROWS, QH * HD), jnp.float32), -6.0, 6.0)
    return noise.astype(jnp.bfloat16)


def block_levels(own_key, shape, pieces, low, largest):
    factor_of, own = 1.0, jax.random.fold_in(own_key, 6)
    for position, blocks in pieces:
        heights = jnp.exp(jax.random.uniform(jax.random.fold_in(own, position), (blocks,), jnp.float32, low / len(pieces), largest / len(pieces)))
        factor_of = factor_of * jnp.repeat(heights, shape[position] // blocks).reshape([-1 if axis == position else 1 for axis in range(len(shape))])
    return factor_of


def split_up(count, total, reach, slope):
    portions = [(1 << 20) // math.isqrt(standing ** slope) + 1 for standing in range(2, count + 1)]
    surplus, given = total - reach - (count - 1), [1] * (count - 1)
    while surplus > 0:
        movable = [i for i in range(count - 1) if given[i] < reach]
        mass, left = sum([portions[i] for i in movable]), surplus
        for i in movable:
            extra = min(reach - given[i], max(1, left * portions[i] // mass), surplus)
            given[i] = given[i] + extra
            surplus = surplus - extra
    return np.array([reach] + given)


def uneven(own_key, count, total, most, skew):
    if count == 2:
        one = jax.random.randint(own_key, (), max(1, total - most), min(most, total - 1) + 1)
        return jnp.stack([one, total - one])
    sizes = jnp.asarray(split_up(count, total, most, skew), jnp.int32)
    twos = (count - 1) // 2
    source_of, taker = sizes[1:1 + 2 * twos:2], sizes[2:2 + 2 * twos:2]
    margin = jnp.minimum(source_of - 1, most - taker)
    passed = jax.random.randint(jax.random.fold_in(own_key, 1), (twos,), 0, 1 << 20) % (margin + 1)
    sizes = sizes.at[1:1 + 2 * twos:2].set(source_of - passed).at[2:2 + 2 * twos:2].set(taker + passed)
    return sizes[jax.random.permutation(jax.random.fold_in(own_key, 2), count)]


def normal_values(own_key, shape, spread, bound, cuts=(), held_as=jnp.bfloat16):
    entries = jax.random.normal(own_key, shape, jnp.float32) * spread
    if len(cuts) > 0:
        entries = block_levels(own_key, shape, cuts, -0.22, 0.18) * entries
    return jnp.clip(entries, min=-bound, max=bound).astype(held_as)


def setup_inputs(seed: int = 0) -> dict:
    key_of = jax.random.split(jax.random.key(seed), 10)
    return {
        "hidden": normal_values(key_of[0], (STEPS, ROWS, D), 1.0, 6.0, ((1, 64),)),
        "queries": draw_queries(jax.random.fold_in(key_of[9], 71), 0),
        "key_cache": draw_key_cache(jax.random.fold_in(key_of[9], 71), 0),
        "value_cache": normal_values(key_of[3], (ROWS, CAP, KVH * HD), 1.0, 6.0, ((0, 64), (2, 8))),
        "lengths": uneven(key_of[4], ROWS, ROWS * CAP * 2 // 5, CAP, 2).astype(jnp.int32),
        "key_gain": jnp.clip(1.0 + 0.15 * jax.random.normal(key_of[5], (HD,), jnp.float32), 0.25, 1.75),
        "base_weight": normal_values(key_of[6], (D, KVH * 2 * HD), D ** -0.5, 0.078125, ((1, 8),)),
        "delta_codes": normal_values(key_of[7], (D, KVH * 2 * HD), 1.0, 4.0, ((0, 512),)),
        "delta_scales": jnp.clip(jnp.exp(math.log(0.049804688) - 2.3038113 * jax.random.uniform(key_of[8], (D, KVH * 2), jnp.float32) ** block_levels(key_of[8], (D, KVH * 2), ((0, 512),), -0.2, 0.2)), 0.0049743652, 0.049804688).astype(jnp.bfloat16),
    }


def rotate_keys(keys, positions):
    half = keys.shape[-1] // 2
    ladder = jnp.arange(half).astype(jnp.float32)
    freqs = jnp.exp(-math.log(1000000.0) * ladder / half)
    angles = positions[..., None] * freqs
    cosine = jnp.cos(angles)
    sine = jnp.sin(angles)
    first = keys[..., :half]
    second = keys[..., half:]
    return jnp.concatenate([first * cosine - second * sine, second * cosine + first * sine], axis=-1)

def make_new(projected, key_gain, lengths, steps):
    width = key_gain.shape[0]
    split = projected.reshape(steps, lengths.shape[0], -1, 2, width)
    keys = split[:, :, :, 0, :]
    values = split[:, :, :, 1, :]
    meansq = lax.optimization_barrier(jnp.mean(keys * keys, axis=-1, keepdims=True))
    keys = keys * lax.rsqrt(meansq + 1e-06) * key_gain
    positions = (lengths[None, :] + jnp.arange(steps)[:, None]).astype(jnp.float32)
    keys = rotate_keys(keys, positions[:, :, None])
    return (keys.astype(jnp.bfloat16), values.astype(jnp.bfloat16))

def attend_row(inputs):
    query_row, cached_keys, cached_values, length, fresh_keys, fresh_values = inputs
    steps, heads, width = fresh_keys.shape
    scale = 1.0 / math.sqrt(width)
    queried = query_row.astype(jnp.float32).reshape(steps, heads, -1, width)
    keyset = cached_keys.astype(jnp.float32).reshape(-1, heads, width)
    valset = cached_values.astype(jnp.float32).reshape(-1, heads, width)
    slots = keyset.shape[0]
    cache_scores = jnp.einsum('skgd,ckd->skgc', queried, keyset) * scale
    valid = jnp.arange(slots) < length
    cache_scores = jnp.where(valid[None, None, None, :], cache_scores, -1e+30)
    fresh_scores = jnp.einsum('skgd,tkd->skgt', queried, fresh_keys.astype(jnp.float32)) * scale
    later = jnp.arange(steps)[None, :] <= jnp.arange(steps)[:, None]
    fresh_scores = jnp.where(later[:, None, None, :], fresh_scores, -1e+30)
    highest = jnp.maximum(lax.optimization_barrier(jnp.max(cache_scores, axis=-1)), lax.optimization_barrier(jnp.max(fresh_scores, axis=-1)))[..., None]
    cache_exp = jnp.exp(cache_scores - highest)
    fresh_exp = jnp.exp(fresh_scores - highest)
    summed = lax.optimization_barrier(jnp.sum(cache_exp, axis=-1, keepdims=True)) + lax.optimization_barrier(jnp.sum(fresh_exp, axis=-1, keepdims=True))
    cache_probs = (cache_exp / summed).astype(jnp.bfloat16).astype(jnp.float32)
    fresh_probs = (fresh_exp / summed).astype(jnp.bfloat16).astype(jnp.float32)
    result = jnp.einsum('skgc,ckd->skgd', cache_probs, valset)
    result = result + jnp.einsum('skgt,tkd->skgd', fresh_probs, fresh_values.astype(jnp.float32))
    return result.reshape(steps, -1).astype(jnp.bfloat16)

def reference(hidden, queries, key_cache, value_cache, lengths, key_gain, base_weight, delta_codes, delta_scales):
    width = key_gain.shape[0]
    factor = jnp.repeat(delta_scales.astype(jnp.float32), width, axis=1)
    weight = (base_weight.astype(jnp.float32) + delta_codes.astype(jnp.float32) * factor).astype(jnp.bfloat16)
    steps = hidden.shape[0]
    flattened = hidden.reshape(-1, hidden.shape[2])
    projected = jnp.dot(flattened, weight, preferred_element_type=jnp.float32)
    fresh_keys, fresh_values = make_new(projected, key_gain, lengths, steps)
    rows_out = lax.map(attend_row, (jnp.transpose(queries, (1, 0, 2)), key_cache, value_cache, lengths, jnp.transpose(fresh_keys, (1, 0, 2, 3)), jnp.transpose(fresh_values, (1, 0, 2, 3))))
    return jnp.transpose(rows_out, (1, 0, 2))
```

```python
import functools
import math

import jax
import jax.numpy as jnp
from jax import lax
from jax.experimental import pallas as pl
from jax.experimental.pallas import tpu as pltpu
from jax.sharding import PartitionSpec as P

MESH = pl.DeviceIdType.MESH
F32 = jnp.float32
BF16 = jnp.bfloat16

STEPS = 3
ROWS = 8
HD = 128
HEADS = 8
CAP = 512
D = 5120
OWNED = 10
CHUNK = 80
WIDE = 256
WINDOW = 384
QROWS = STEPS * HEADS
ALLQ = ROWS * QROWS
FRESH = STEPS * ROWS
EARLY = 4


def iota(shape, dim):
    return lax.broadcasted_iota(jnp.int32, shape, dim)


def dot(a, b):
    return jnp.dot(a, b, preferred_element_type=F32)


def dot_t(a, b):
    return lax.dot_general(a, b, (((1,), (1,)), ((), ())), preferred_element_type=F32)


def swap_matrix():
    shape = (8, STEPS, 8, ALLQ)
    hit = iota(shape, 3) == iota(shape, 2) * QROWS + iota(shape, 1) * 8 + iota(shape, 0)
    return jnp.where(hit, 1.0, 0.0).astype(F32).reshape(ALLQ, ALLQ).astype(BF16)


def kernel(
    lengths_hbm, gain_hbm, codes_hbm, scales_hbm, base_hbm, hidden_hbm, queries_hbm, kc_hbm, vc_hbm,
    out_ref,
    lens, gain, codes, scales, basebuf, qbuf, kc, vc,
    msg, inbox, wbuf, hbuf, pout, pin, qall, acc, mbuf, lbuf, cosb, sinb,
    local_sem, own_sem, s1, r1, sh, rh, s2, r2, s3, r3,
):
    g = lax.axis_index("group")
    t = lax.axis_index("tp")
    ci = lax.rem(lax.div(g, 16), 2) * 4 + lax.rem(g, 4)
    b = lax.div(g, 32) * 4 + lax.rem(lax.div(g, 4), 4)

    def group_of(c, m):
        return lax.div(m, 4) * 32 + lax.div(c, 4) * 16 + lax.rem(m, 4) * 4 + lax.rem(c, 4)

    def window(m, half):
        q = lax.div(m, 4) * 8 + half * 4 + lax.rem(m, 4)
        return pl.ds(pl.multiple_of(q * 320 - lax.rem(m, 2) * 64, 128), WINDOW)

    def other(mine, k):
        return lax.rem(mine + k, 8)

    loads = [
        pltpu.make_async_copy(src, dst, local_sem.at[i])
        for i, (src, dst) in enumerate(
            [
                (codes_hbm, codes),
                (scales_hbm, scales),
                (lengths_hbm, lens),
                (queries_hbm, qbuf),
                (gain_hbm, gain),
                (base_hbm.at[pl.ds(pl.multiple_of(g * CHUNK, 16), CHUNK), :], basebuf),
                (kc_hbm, kc),
                (vc_hbm, vc),
            ]
        )
    ]
    for load in loads:
        load.start()
    own_hidden = [
        pltpu.make_async_copy(hidden_hbm.at[:, :, window(b, half)], hbuf.at[b, half], own_sem.at[half])
        for half in range(2)
    ]
    for copy in own_hidden:
        copy.start()

    wbuf[:, pl.ds(pl.multiple_of(320 * (1 - lax.rem(b, 2)), 64), 64), :] = jnp.zeros((2, 64, WIDE), BF16)

    barrier = pltpu.get_barrier_semaphore()
    for k in range(1, 8):
        pl.semaphore_signal(barrier, inc=1, device_id=(g, other(t, k)), device_id_type=MESH)
    for k in range(1, 8):
        pl.semaphore_signal(barrier, inc=1, device_id=(group_of(ci, other(b, k)), t), device_id_type=MESH)
    for k in range(1, 8):
        pl.semaphore_signal(barrier, inc=1, device_id=(group_of(other(ci, k), b), t), device_id_type=MESH)

    msg[...] = jnp.zeros((8, 16, WIDE + 128), BF16)
    loads[0].wait()
    loads[1].wait()
    for k in range(8):
        msg[k, 0:OWNED, 0:WIDE] = codes[:, k * WIDE : (k + 1) * WIDE]
        msg[k, 0:OWNED, WIDE : WIDE + 16] = scales[...]

    pl.semaphore_wait(barrier, 21)

    def to_rank(k):
        peer = other(t, k)
        return pltpu.make_async_remote_copy(
            msg.at[peer], inbox.at[t], s1.at[k], r1.at[t], device_id=(g, peer), device_id_type=MESH
        )

    def from_rank(k):
        peer = other(t, k)
        return pltpu.make_async_remote_copy(
            msg.at[t], inbox.at[peer], s1.at[k], r1.at[peer], device_id=(g, peer), device_id_type=MESH
        )

    def hidden_out(k, half):
        peer = other(b, k)
        return pltpu.make_async_remote_copy(
            hidden_hbm.at[:, :, window(peer, half)],
            hbuf.at[b, half],
            sh.at[k, half],
            rh.at[b, half],
            device_id=(group_of(ci, peer), t),
            device_id_type=MESH,
        )

    def hidden_in(k, half):
        peer = other(b, k)
        return pltpu.make_async_remote_copy(
            hidden_hbm.at[:, :, window(b, half)],
            hbuf.at[peer, half],
            sh.at[k, half],
            rh.at[peer, half],
            device_id=(group_of(ci, peer), t),
            device_id_type=MESH,
        )

    def place(c):
        return wbuf.at[lax.div(c, 4), pl.ds(pl.multiple_of(64 * lax.rem(b, 2) + CHUNK * lax.rem(c, 4), 16), CHUNK), :]

    def weight_copy(k, owner):
        peer = other(ci, k)
        return pltpu.make_async_remote_copy(
            place(owner), place(owner), s2.at[k], r2.at[owner],
            device_id=(group_of(peer, b), t), device_id_type=MESH,
        )

    def sum_out(k):
        peer = other(b, k)
        return pltpu.make_async_remote_copy(
            pout.at[peer], pin.at[b], s3.at[k], r3.at[b], device_id=(group_of(ci, peer), t), device_id_type=MESH
        )

    def sum_in(k):
        peer = other(b, k)
        return pltpu.make_async_remote_copy(
            pout.at[b], pin.at[peer], s3.at[k], r3.at[peer], device_id=(group_of(ci, peer), t), device_id_type=MESH
        )

    for k in range(1, 8):
        to_rank(k).start()
    for k in range(1, 8):
        for half in range(2):
            hidden_out(k, half).start()
    inbox[t] = msg[t]

    loads[3].wait()
    swap = swap_matrix()
    flat = qbuf[...].astype(F32).reshape(FRESH, HEADS * HD)
    stacked = jnp.concatenate([flat[:, h * HD : (h + 1) * HD] for h in range(HEADS)], axis=0)
    qall[...] = dot(swap, stacked.astype(BF16))

    loads[2].wait()
    lane = iota((ROWS, HD), 1)
    row = iota((ROWS, HD), 0)
    start = jnp.zeros((ROWS, HD), F32)
    for r in range(ROWS):
        start = jnp.where(row == r, lens[r].astype(F32), start)
    ladder = jnp.where(lane < HD // 2, lane, lane - HD // 2).astype(F32)
    freqs = jnp.exp(-math.log(1000000.0) * ladder / (HD // 2))
    for s in range(STEPS):
        angles = (start + float(s)) * freqs
        cosb[s * ROWS : (s + 1) * ROWS, :] = jnp.cos(angles)
        sine = jnp.sin(angles)
        sinb[s * ROWS : (s + 1) * ROWS, :] = jnp.where(lane < HD // 2, -sine, sine)

    loads[6].wait()
    loads[7].wait()
    scale = 1.0 / math.sqrt(HD)

    def attend(r, carry):
        rows = pl.ds(pl.multiple_of(r * QROWS, 8), QROWS)
        scores = dot_t(qall[rows, :].astype(BF16), kc[r]) * scale
        scores = jnp.where(iota((QROWS, CAP), 1) < lens[r], scores, -1e30)
        highest = jnp.max(scores, axis=-1, keepdims=True)
        weights = jnp.exp(scores - highest)
        mbuf[rows, :] = jnp.broadcast_to(highest, (QROWS, HD))
        lbuf[rows, :] = jnp.broadcast_to(jnp.sum(weights, axis=-1, keepdims=True), (QROWS, HD))
        acc[rows, :] = dot(weights.astype(BF16), vc[r])
        return carry

    lax.fori_loop(0, EARLY, attend, 0)

    loads[4].wait()
    loads[5].wait()
    for k in range(1, 8):
        from_rank(k).wait_recv()
    i = iota((CHUNK, 128), 0)
    packed = i + 6 * lax.shift_right_logical(i * 205, 11)
    pick = jnp.where(iota((CHUNK, 128), 1) == packed, 1.0, 0.0).astype(BF16)
    got = dot(pick, inbox[...].reshape(128, WIDE + 128))
    half_of = jnp.where(iota((128, WIDE), 1) >= HD, 1, 0)
    spread = jnp.where(iota((128, WIDE), 0) == 2 * t + half_of, 1.0, 0.0).astype(BF16)
    factor = dot(got[:, WIDE:].astype(BF16), spread)
    place(ci)[...] = (basebuf[...].astype(F32) + got[:, :WIDE] * factor).astype(BF16)
    for k in range(1, 8):
        weight_copy(k, ci).start()

    lax.fori_loop(EARLY, ROWS, attend, 0)

    for copy in own_hidden:
        copy.wait()
    for k in range(1, 8):
        for half in range(2):
            hidden_in(k, half).wait_recv()
    lefts = [hbuf[:, half].astype(F32).reshape(8 * FRESH, WINDOW).astype(BF16) for half in range(2)]
    for k in range(1, 8):
        weight_copy(k, other(ci, k)).wait_recv()
    partial = dot(lefts[0], wbuf[0]) + dot(lefts[1], wbuf[1])
    pout[...] = partial.reshape(8, FRESH, WIDE)
    for k in range(1, 8):
        sum_out(k).start()
    pin[b] = pout[b]
    swap = swap_matrix()
    everything = qall[...].astype(BF16)
    shape = (ROWS, STEPS, HEADS, FRESH)
    col = iota(shape, 3)
    slot = jnp.where(col >= 2 * ROWS, 2, jnp.where(col >= ROWS, 1, 0))
    seen = (col - slot * ROWS == iota(shape, 0)) & (slot <= iota(shape, 1))
    bias = jnp.where(seen, 0.0, -1e30).astype(F32).reshape(ALLQ, FRESH)
    for k in range(1, 8):
        sum_in(k).wait_recv()
    projected = pin[0]
    for m in range(1, 8):
        projected = projected + pin[m]

    keys = projected[:, :HD]
    meansq = jnp.mean(keys * keys, axis=-1, keepdims=True)
    keys = keys * lax.rsqrt(meansq + 1e-06) * gain[...]
    turned = jnp.concatenate([keys[:, HD // 2 :], keys[:, : HD // 2]], axis=1)
    keys = (keys * cosb[...] + turned * sinb[...]).astype(BF16)
    values = projected[:, HD:].astype(BF16)

    scores = dot_t(everything, keys) * scale + bias
    before = mbuf[...]
    highest = jnp.maximum(before[:, :1], jnp.max(scores, axis=-1, keepdims=True))
    weights = jnp.exp(scores - highest)
    shrink = jnp.exp(before - highest)
    total = shrink * lbuf[...] + jnp.sum(weights, axis=-1, keepdims=True)
    result = (shrink * acc[...] + dot(weights.astype(BF16), values)) / total
    result = dot(swap, result.astype(BF16))
    result = jnp.concatenate([result[h * FRESH : (h + 1) * FRESH, :] for h in range(HEADS)], axis=1)
    out_ref[...] = result.reshape(STEPS, ROWS, HEADS * HD).astype(BF16)

    for k in range(1, 8):
        to_rank(k).wait_send()
        for half in range(2):
            hidden_out(k, half).wait_send()
        weight_copy(k, ci).wait_send()
        sum_out(k).wait_send()


def per_device(hidden, queries, key_cache, value_cache, lengths, key_gain, base_weight, delta_codes, delta_scales):
    dma = pltpu.SemaphoreType.DMA
    return pl.pallas_call(
        kernel,
        out_shape=jax.ShapeDtypeStruct((STEPS, ROWS, HEADS * HD), BF16),
        in_specs=[pl.BlockSpec(memory_space=pl.ANY)] * 9,
        out_specs=pl.BlockSpec(memory_space=pltpu.VMEM),
        scratch_shapes=[
            pltpu.SMEM((ROWS,), jnp.int32),
            pltpu.VMEM((1, HD), F32),
            pltpu.VMEM((OWNED, 8 * WIDE), BF16),
            pltpu.VMEM((OWNED, 16), BF16),
            pltpu.VMEM((CHUNK, WIDE), BF16),
            pltpu.VMEM((STEPS, ROWS, HEADS * HD), BF16),
            pltpu.VMEM((ROWS, CAP, HD), BF16),
            pltpu.VMEM((ROWS, CAP, HD), BF16),
            pltpu.VMEM((8, 16, WIDE + 128), BF16),
            pltpu.VMEM((8, 16, WIDE + 128), BF16),
            pltpu.VMEM((2, WINDOW, WIDE), BF16),
            pltpu.VMEM((8, 2, STEPS, ROWS, WINDOW), BF16),
            pltpu.VMEM((8, FRESH, WIDE), F32),
            pltpu.VMEM((8, FRESH, WIDE), F32),
            pltpu.VMEM((ALLQ, HD), F32),
            pltpu.VMEM((ALLQ, HD), F32),
            pltpu.VMEM((ALLQ, HD), F32),
            pltpu.VMEM((ALLQ, HD), F32),
            pltpu.VMEM((FRESH, HD), F32),
            pltpu.VMEM((FRESH, HD), F32),
            dma((8,)), dma((2,)),
            dma((8,)), dma((8,)),
            dma((8, 2)), dma((8, 2)),
            dma((8,)), dma((8,)),
            dma((8,)), dma((8,)),
        ],
        compiler_params=pltpu.CompilerParams(
            collective_id=0, has_side_effects=True, vmem_limit_bytes=56 * 1024 * 1024
        ),
        name="project_and_attend",
    )(
        lengths, key_gain.reshape(1, HD), delta_codes, delta_scales, base_weight, hidden, queries, key_cache, value_cache,
    )


def solution(mesh):
    return jax.shard_map(
        per_device,
        mesh=mesh,
        in_specs=(
            P(None, "group", None),
            P(None, "group", "tp"),
            P("group", None, "tp"),
            P("group", None, "tp"),
            P("group"),
            P(),
            P(None, "tp"),
            P(("group", "tp"), None),
            P(("group", "tp"), None),
        ),
        out_specs=P(None, "group", "tp"),
        check_vma=False,
    )
```

```python
import functools
import math

import jax
import jax.numpy as jnp
from jax import lax
from jax.experimental import pallas as pl
from jax.experimental.pallas import tpu as pltpu
from jax.sharding import PartitionSpec as P

MESH = pl.DeviceIdType.MESH
F32 = jnp.float32
BF16 = jnp.bfloat16

STEPS = 3
ROWS = 8
HD = 128
HEADS = 8
CAP = 512
D = 5120
OWNED = 10
CHUNK = 80
WIDE = 256
WINDOW = 384
QROWS = STEPS * HEADS
ALLQ = ROWS * QROWS
FRESH = STEPS * ROWS
EARLY = 4


def iota(shape, dim):
    return lax.broadcasted_iota(jnp.int32, shape, dim)


def dot(a, b):
    return jnp.dot(a, b, preferred_element_type=F32)


def dot_t(a, b):
    return lax.dot_general(a, b, (((1,), (1,)), ((), ())), preferred_element_type=F32)


def swap_matrix():
    shape = (8, STEPS, 8, ALLQ)
    hit = iota(shape, 3) == iota(shape, 2) * QROWS + iota(shape, 1) * 8 + iota(shape, 0)
    return jnp.where(hit, 1.0, 0.0).astype(F32).reshape(ALLQ, ALLQ).astype(BF16)


def kernel(
    lengths_hbm, gain_hbm, codes_hbm, scales_hbm, base_hbm, hidden_hbm, queries_hbm, kc_hbm, vc_hbm,
    out_ref,
    lens, gain, codes, scales, basebuf, qbuf, kc, vc,
    msg, inbox, packed, arrived, wbuf, hbuf, pout, pin, qall, acc, mbuf, lbuf, cosb, sinb,
    local_sem, base_sem, own_sem, s1, r1, sh, rh, s2, r2, sf, rf, s3, r3,
):
    g = lax.axis_index("group")
    t = lax.axis_index("tp")
    core = lax.rem(g, 2)
    y0 = lax.rem(lax.div(g, 2), 2)
    y1 = lax.rem(lax.div(g, 4), 2)
    y2 = lax.rem(lax.div(g, 8), 2)
    z0 = lax.rem(lax.div(g, 16), 2)
    z1 = lax.div(g, 32)
    x, zh = lax.div(t, 2), lax.rem(t, 2)
    b = z1 * 4 + y2 * 2 + y1

    def peer_x(k):
        return lax.rem(x + k, 4)

    def member(m):
        return lax.div(m, 4) * 32 + z0 * 16 + lax.rem(m, 4) * 4 + y0 * 2 + core

    def across(j):
        return (1 - z1) * 32 + (j // 2) * 16 + y2 * 8 + y1 * 4 + (j % 2) * 2 + core

    sibling = g + 1 - 2 * core

    def window(m, half):
        q = (1 - lax.div(m, 4)) * 8 + half * 4 + lax.rem(m, 4)
        return pl.ds(pl.multiple_of(q * 320 - lax.rem(m, 2) * 64, 128), WINDOW)

    def other(mine, k):
        return lax.rem(mine + k, 8)

    loads = [
        pltpu.make_async_copy(src, dst, local_sem.at[i])
        for i, (src, dst) in enumerate(
            [
                (codes_hbm, codes),
                (scales_hbm, scales),
                (lengths_hbm, lens),
                (queries_hbm, qbuf),
                (gain_hbm, gain),
                (kc_hbm, kc),
                (vc_hbm, vc),
            ]
        )
    ]
    base_loads = [
        pltpu.make_async_copy(
            base_hbm.at[pl.ds(pl.multiple_of(across(j) * CHUNK, 16), CHUNK), :], basebuf.at[j], base_sem.at[j]
        )
        for j in range(4)
    ]
    own_hidden = [
        pltpu.make_async_copy(hidden_hbm.at[:, :, window(b, half)], hbuf.at[b, half], own_sem.at[half])
        for half in range(2)
    ]

    barrier = pltpu.get_barrier_semaphore()
    loads[0].start()
    loads[1].start()
    for k in range(1, 4):
        pl.semaphore_signal(barrier, inc=1, device_id=(g, peer_x(k) * 2 + zh), device_id_type=MESH)
    for j in range(4):
        for half in range(2):
            pl.semaphore_signal(barrier, inc=1, device_id=(across(j), x * 2 + half), device_id_type=MESH)
    for k in range(1, 8):
        pl.semaphore_signal(barrier, inc=1, device_id=(member(other(b, k)), t), device_id_type=MESH)
    pl.semaphore_signal(barrier, inc=1, device_id=(sibling, t), device_id_type=MESH)
    for load in loads[2:]:
        load.start()
    for load in own_hidden + base_loads:
        load.start()

    msg[...] = jnp.zeros(msg.shape, BF16)
    loads[0].wait()
    loads[1].wait()
    for k in range(4):
        msg[k, 0:OWNED, 0 : 2 * WIDE] = codes[:, k * 2 * WIDE : (k + 1) * 2 * WIDE]
        msg[k, 0:OWNED, 2 * WIDE : 2 * WIDE + 16] = scales[...]

    def to_x(k):
        return pltpu.make_async_remote_copy(
            msg.at[peer_x(k)], inbox.at[x], s1.at[k], r1.at[x],
            device_id=(g, peer_x(k) * 2 + zh), device_id_type=MESH,
        )

    def from_x(k):
        return pltpu.make_async_remote_copy(
            msg.at[x], inbox.at[peer_x(k)], s1.at[k], r1.at[peer_x(k)],
            device_id=(g, peer_x(k) * 2 + zh), device_id_type=MESH,
        )

    def hidden_out(k, half):
        peer = other(b, k)
        return pltpu.make_async_remote_copy(
            hidden_hbm.at[:, :, window(peer, half)], hbuf.at[b, half], sh.at[k, half], rh.at[b, half],
            device_id=(member(peer), t), device_id_type=MESH,
        )

    def hidden_in(k, half):
        peer = other(b, k)
        return pltpu.make_async_remote_copy(
            hidden_hbm.at[:, :, window(b, half)], hbuf.at[peer, half], sh.at[k, half], rh.at[peer, half],
            device_id=(member(peer), t), device_id_type=MESH,
        )

    def codes_out(j, half):
        source = (z0 * 2 + y0) * 2 + zh
        return pltpu.make_async_remote_copy(
            packed.at[half], arrived.at[source], s2.at[2 * j + half], r2.at[source],
            device_id=(across(j), x * 2 + half), device_id_type=MESH,
        )

    def codes_in(j, half):
        return pltpu.make_async_remote_copy(
            packed.at[half], arrived.at[2 * j + half], s2.at[2 * j + half], r2.at[2 * j + half],
            device_id=(across(j), x * 2 + half), device_id_type=MESH,
        )

    def place(j, c):
        return wbuf.at[j // 2, pl.ds(pl.multiple_of(64 * y1 + CHUNK * (2 * (j % 2) + c), 16), CHUNK), :]

    def weight_copy(j, c):
        return pltpu.make_async_remote_copy(
            place(j, c), place(j, c), sf.at[j], rf.at[j], device_id=(sibling, t), device_id_type=MESH
        )

    def sum_out(k):
        peer = other(b, k)
        return pltpu.make_async_remote_copy(
            pout.at[peer], pin.at[b], s3.at[k], r3.at[b], device_id=(member(peer), t), device_id_type=MESH
        )

    def sum_in(k):
        peer = other(b, k)
        return pltpu.make_async_remote_copy(
            pout.at[b], pin.at[peer], s3.at[k], r3.at[peer], device_id=(member(peer), t), device_id_type=MESH
        )

    pl.semaphore_wait(barrier, 19)
    for k in range(1, 4):
        to_x(k).start()
    for k in range(1, 8):
        for half in range(2):
            hidden_out(k, half).start()
    inbox[x] = msg[x]

    wbuf[:, pl.ds(pl.multiple_of(320 * (1 - y1), 64), 64), :] = jnp.zeros((2, 64, WIDE), BF16)

    loads[3].wait()
    swap = swap_matrix()
    flat = qbuf[...].astype(F32).reshape(FRESH, HEADS * HD)
    stacked = jnp.concatenate([flat[:, h * HD : (h + 1) * HD] for h in range(HEADS)], axis=0)
    qall[...] = dot(swap, stacked.astype(BF16))

    loads[2].wait()
    lane = iota((ROWS, HD), 1)
    row = iota((ROWS, HD), 0)
    start = jnp.zeros((ROWS, HD), F32)
    for r in range(ROWS):
        start = jnp.where(row == r, lens[r].astype(F32), start)
    ladder = jnp.where(lane < HD // 2, lane, lane - HD // 2).astype(F32)
    freqs = jnp.exp(-math.log(1000000.0) * ladder / (HD // 2))
    for s in range(STEPS):
        angles = (start + float(s)) * freqs
        cosb[s * ROWS : (s + 1) * ROWS, :] = jnp.cos(angles)
        sine = jnp.sin(angles)
        sinb[s * ROWS : (s + 1) * ROWS, :] = jnp.where(lane < HD // 2, -sine, sine)

    loads[5].wait()
    loads[6].wait()
    scale = 1.0 / math.sqrt(HD)

    def attend(r, carry):
        rows = pl.ds(pl.multiple_of(r * QROWS, 8), QROWS)
        scores = dot_t(qall[rows, :].astype(BF16), kc[r]) * scale
        scores = jnp.where(iota((QROWS, CAP), 1) < lens[r], scores, -1e30)
        highest = jnp.max(scores, axis=-1, keepdims=True)
        weights = jnp.exp(scores - highest)
        mbuf[rows, :] = jnp.broadcast_to(highest, (QROWS, HD))
        lbuf[rows, :] = jnp.broadcast_to(jnp.sum(weights, axis=-1, keepdims=True), (QROWS, HD))
        acc[rows, :] = dot(weights.astype(BF16), vc[r])
        return carry

    lax.fori_loop(0, EARLY, attend, 0)

    i = iota((40, 64), 0)
    tens = lax.shift_right_logical(i * 205, 11)
    pick = jnp.where(iota((40, 64), 1) == i + 6 * tens, 1.0, 0.0).astype(BF16)
    i = iota((16, 128), 0)
    column = 4 * x + jnp.where(i < 8, i, i - 6)
    wanted = (iota((16, 128), 1) == column) & ((i < 2) | ((i >= 8) & (i < 10)))
    choose = jnp.where(wanted, 1.0, 0.0).astype(BF16)
    for k in range(1, 4):
        from_x(k).wait_recv()
    got = inbox[...].reshape(64, 2 * WIDE + 128)
    factors = dot_t(choose, jnp.concatenate([got[:, 2 * WIDE :], jnp.zeros((64, 128), BF16)], axis=0))
    body = dot(pick, got[:, : 2 * WIDE])
    for half in range(2):
        last = jnp.concatenate([factors[8 * half : 8 * half + 8, :], jnp.zeros((8, 128), F32)], axis=1)
        whole = jnp.concatenate([body[:, half * WIDE : (half + 1) * WIDE], last], axis=0)
        packed[half] = whole.astype(BF16)
    for half in range(2):
        for j in range(4):
            codes_out(j, half).start()

    lax.fori_loop(EARLY, ROWS, attend, 0)

    for load in base_loads:
        load.wait()
    i = iota((CHUNK, 96), 0)
    tens = lax.shift_right_logical(i * 205, 11)
    odd = lax.rem(tens, 2)
    within = i - 10 * tens
    pair = lax.div(tens, 2)
    pick = jnp.where(iota((CHUNK, 96), 1) == odd * 48 + pair * 10 + within, 1.0, 0.0).astype(BF16)
    i = iota((CHUNK, 256), 0)
    tens = lax.shift_right_logical(i * 205, 11)
    odd = lax.rem(tens, 2)
    within = i - 10 * tens
    pair = lax.div(tens, 2)
    spread = jnp.where(iota((CHUNK, 256), 1) == odd * 128 + pair * 16 + within, 1.0, 0.0).astype(BF16)
    for j in range(4):
        for half in range(2):
            codes_in(j, half).wait_recv()
        both = arrived[2 * j : 2 * j + 2].reshape(96, WIDE)
        update = dot(pick, both)
        columns = []
        for half in range(2):
            ends = arrived[2 * j + half, 32:48, 0:128].astype(F32)
            columns.append(
                jnp.concatenate(
                    [jnp.broadcast_to(ends[8 + part : 9 + part, :], (128, 128)) for part in range(2)], axis=0
                )
            )
        factor = dot_t(spread, jnp.concatenate(columns, axis=1).astype(BF16))
        place(j, core)[...] = (basebuf[j].astype(F32) + update * factor).astype(BF16)
        weight_copy(j, core).start()

    for copy in own_hidden:
        copy.wait()
    for k in range(1, 8):
        for half in range(2):
            hidden_in(k, half).wait_recv()
    lefts = [hbuf[:, half].astype(F32).reshape(8 * FRESH, WINDOW).astype(BF16) for half in range(2)]
    loads[4].wait()
    for j in range(4):
        weight_copy(j, 1 - core).wait_recv()
    partial = dot(lefts[0], wbuf[0]) + dot(lefts[1], wbuf[1])
    pout[...] = partial.reshape(8, FRESH, WIDE)
    for k in range(1, 8):
        sum_out(k).start()
    pin[b] = pout[b]
    swap = swap_matrix()
    everything = qall[...].astype(BF16)
    shape = (ROWS, STEPS, HEADS, FRESH)
    col = iota(shape, 3)
    slot = jnp.where(col >= 2 * ROWS, 2, jnp.where(col >= ROWS, 1, 0))
    seen = (col - slot * ROWS == iota(shape, 0)) & (slot <= iota(shape, 1))
    bias = jnp.where(seen, 0.0, -1e30).astype(F32).reshape(ALLQ, FRESH)
    for k in range(1, 8):
        sum_in(k).wait_recv()
    projected = pin[0]
    for m in range(1, 8):
        projected = projected + pin[m]

    keys = projected[:, :HD]
    meansq = jnp.mean(keys * keys, axis=-1, keepdims=True)
    keys = keys * lax.rsqrt(meansq + 1e-06) * gain[...]
    turned = jnp.concatenate([keys[:, HD // 2 :], keys[:, : HD // 2]], axis=1)
    keys = (keys * cosb[...] + turned * sinb[...]).astype(BF16)
    values = projected[:, HD:].astype(BF16)

    scores = dot_t(everything, keys) * scale + bias
    before = mbuf[...]
    highest = jnp.maximum(before[:, :1], jnp.max(scores, axis=-1, keepdims=True))
    weights = jnp.exp(scores - highest)
    shrink = jnp.exp(before - highest)
    total = shrink * lbuf[...] + jnp.sum(weights, axis=-1, keepdims=True)
    result = (shrink * acc[...] + dot(weights.astype(BF16), values)) / total
    result = dot(swap, result.astype(BF16))
    result = jnp.concatenate([result[h * FRESH : (h + 1) * FRESH, :] for h in range(HEADS)], axis=1)
    out_ref[...] = result.reshape(STEPS, ROWS, HEADS * HD).astype(BF16)

    for k in range(1, 4):
        to_x(k).wait_send()
    for j in range(4):
        for half in range(2):
            codes_out(j, half).wait_send()
        weight_copy(j, core).wait_send()
    for k in range(1, 8):
        for half in range(2):
            hidden_out(k, half).wait_send()
        sum_out(k).wait_send()


def per_device(hidden, queries, key_cache, value_cache, lengths, key_gain, base_weight, delta_codes, delta_scales):
    dma = pltpu.SemaphoreType.DMA
    return pl.pallas_call(
        kernel,
        out_shape=jax.ShapeDtypeStruct((STEPS, ROWS, HEADS * HD), BF16),
        in_specs=[pl.BlockSpec(memory_space=pl.ANY)] * 9,
        out_specs=pl.BlockSpec(memory_space=pltpu.VMEM),
        scratch_shapes=[
            pltpu.SMEM((ROWS,), jnp.int32),
            pltpu.VMEM((1, HD), F32),
            pltpu.VMEM((OWNED, 8 * WIDE), BF16),
            pltpu.VMEM((OWNED, 16), BF16),
            pltpu.VMEM((4, CHUNK, WIDE), BF16),
            pltpu.VMEM((STEPS, ROWS, HEADS * HD), BF16),
            pltpu.VMEM((ROWS, CAP, HD), BF16),
            pltpu.VMEM((ROWS, CAP, HD), BF16),
            pltpu.VMEM((4, 16, 2 * WIDE + 128), BF16),
            pltpu.VMEM((4, 16, 2 * WIDE + 128), BF16),
            pltpu.VMEM((2, 48, WIDE), BF16),
            pltpu.VMEM((8, 48, WIDE), BF16),
            pltpu.VMEM((2, WINDOW, WIDE), BF16),
            pltpu.VMEM((8, 2, STEPS, ROWS, WINDOW), BF16),
            pltpu.VMEM((8, FRESH, WIDE), F32),
            pltpu.VMEM((8, FRESH, WIDE), F32),
            pltpu.VMEM((ALLQ, HD), F32),
            pltpu.VMEM((ALLQ, HD), F32),
            pltpu.VMEM((ALLQ, HD), F32),
            pltpu.VMEM((ALLQ, HD), F32),
            pltpu.VMEM((FRESH, HD), F32),
            pltpu.VMEM((FRESH, HD), F32),
            dma((7,)), dma((4,)), dma((2,)),
            dma((4,)), dma((4,)),
            dma((8, 2)), dma((8, 2)),
            dma((8,)), dma((8,)),
            dma((4,)), dma((4,)),
            dma((8,)), dma((8,)),
        ],
        compiler_params=pltpu.CompilerParams(
            collective_id=0, has_side_effects=True, vmem_limit_bytes=56 * 1024 * 1024
        ),
        name="project_and_attend",
    )(
        lengths, key_gain.reshape(1, HD), delta_codes, delta_scales, base_weight, hidden, queries, key_cache, value_cache,
    )


def solution(mesh):
    return jax.shard_map(
        per_device,
        mesh=mesh,
        in_specs=(
            P(None, "group", None),
            P(None, "group", "tp"),
            P("group", None, "tp"),
            P("group", None, "tp"),
            P("group"),
            P(),
            P(None, "tp"),
            P(("group", "tp"), None),
            P(("group", "tp"), None),
        ),
        out_specs=P(None, "group", "tp"),
        check_vma=False,
    )
```

```python
import functools
import math

import jax
import jax.numpy as jnp
from jax import lax
from jax.experimental import pallas as pl
from jax.experimental.pallas import tpu as pltpu
from jax.sharding import PartitionSpec as P

MESH = pl.DeviceIdType.MESH
F32 = jnp.float32
BF16 = jnp.bfloat16

STEPS = 3
ROWS = 8
HD = 128
HEADS = 8
CAP = 512
D = 5120
OWNED = 10
CHUNK = 80
WIDE = 256
SLICE = D // 8
FAR_FIRST = (4, 3, 5, 2, 6, 1, 7)
QROWS = STEPS * HEADS
ALLQ = ROWS * QROWS
FRESH = STEPS * ROWS
EARLY = 3


def iota(shape, dim):
    return lax.broadcasted_iota(jnp.int32, shape, dim)


def dot(a, b):
    return jnp.dot(a, b, preferred_element_type=F32)


def dot_t(a, b):
    return lax.dot_general(a, b, (((1,), (1,)), ((), ())), preferred_element_type=F32)


def swap_matrix():
    shape = (8, STEPS, 8, ALLQ)
    hit = iota(shape, 3) == iota(shape, 2) * QROWS + iota(shape, 1) * 8 + iota(shape, 0)
    return jnp.where(hit, 1.0, 0.0).astype(F32).reshape(ALLQ, ALLQ).astype(BF16)


def kernel(
    lengths_hbm, gain_hbm, codes_hbm, scales_hbm, base_hbm, hidden_hbm, queries_hbm, kc_hbm, vc_hbm,
    out_ref,
    lens, gain, basebuf, qbuf, hfull, kc, vc,
    boxc, boxs, inbox, packed, arrived, wbuf, hsend, hbuf, pout, pin, qall, acc, mbuf, lbuf, cosb, sinb,
    local_sem, base_sem, s1, r1, sh, rh, s2, r2, sf, rf, s3, r3,
):
    g = lax.axis_index("group")
    t = lax.axis_index("tp")
    core = lax.rem(g, 2)
    y = lax.rem(lax.div(g, 2), 8)
    zl = lax.div(g, 16)
    x, zh = lax.div(t, 2), lax.rem(t, 2)
    z = zh * 4 + zl

    def peer_x(k):
        return lax.rem(x + k, 4)

    def along_y(k):
        return zl * 16 + other(y, k) * 2 + core

    def along_z(k):
        there = other(z, k)
        return lax.rem(there, 4) * 16 + y * 2 + core, x * 2 + lax.div(there, 4)

    sibling = g + 1 - 2 * core

    def other(mine, k):
        return lax.rem(mine + k, 8)

    loads = [
        pltpu.make_async_copy(src, dst, local_sem.at[i])
        for i, (src, dst) in enumerate(
            [
                (hidden_hbm, hfull),
                (codes_hbm.at[:, pl.ds(pl.multiple_of(x * 2 * WIDE, 128), 2 * WIDE)], boxc.at[x]),
                (scales_hbm, boxs.at[x]),
                (lengths_hbm, lens),
                (queries_hbm, qbuf),
                (gain_hbm, gain),
                (kc_hbm, kc),
                (vc_hbm, vc),
            ]
        )
    ]
    hidden_load, code_load, scale_load, length_load, query_load, gain_load, key_load, value_load = loads
    base_loads = [
        pltpu.make_async_copy(
            base_hbm.at[pl.ds(pl.multiple_of((16 * j + 2 * y + core) * CHUNK, 16), CHUNK), :],
            basebuf.at[j],
            base_sem.at[j],
        )
        for j in range(4)
    ]

    barrier = pltpu.get_barrier_semaphore()
    hidden_load.start()
    for k in range(1, 4):
        pl.semaphore_signal(barrier, inc=1, device_id=(g, peer_x(k) * 2 + zh), device_id_type=MESH)
    for k in FAR_FIRST:
        pl.semaphore_signal(barrier, inc=1, device_id=along_z(k), device_id_type=MESH)
        pl.semaphore_signal(barrier, inc=1, device_id=(along_y(k), t), device_id_type=MESH)
    pl.semaphore_signal(barrier, inc=1, device_id=(sibling, t), device_id_type=MESH)
    for load in loads[1:] + base_loads:
        load.start()

    inbox[...] = jnp.zeros(inbox.shape, BF16)
    hidden_load.wait()
    everything = hfull[...].astype(F32).reshape(FRESH, D)
    for m in range(8):
        columns = [everything[:, j * 1280 + m * 160 : j * 1280 + m * 160 + 160] for j in range(4)]
        hsend[m] = jnp.concatenate(columns, axis=1).reshape(STEPS, ROWS, SLICE).astype(BF16)

    def to_x(k):
        peer = peer_x(k)
        device = (g, peer * 2 + zh)
        return (
            pltpu.make_async_remote_copy(
                codes_hbm.at[:, pl.ds(pl.multiple_of(peer * 2 * WIDE, 128), 2 * WIDE)], boxc.at[x],
                s1.at[k, 0], r1.at[x, 0], device_id=device, device_id_type=MESH,
            ),
            pltpu.make_async_remote_copy(
                scales_hbm, boxs.at[x], s1.at[k, 1], r1.at[x, 1], device_id=device, device_id_type=MESH
            ),
        )

    def from_x(k):
        peer = peer_x(k)
        device = (g, peer * 2 + zh)
        return (
            pltpu.make_async_remote_copy(
                codes_hbm.at[:, pl.ds(pl.multiple_of(x * 2 * WIDE, 128), 2 * WIDE)], boxc.at[peer],
                s1.at[k, 0], r1.at[peer, 0], device_id=device, device_id_type=MESH,
            ),
            pltpu.make_async_remote_copy(
                scales_hbm, boxs.at[peer], s1.at[k, 1], r1.at[peer, 1], device_id=device, device_id_type=MESH
            ),
        )

    def hidden_out(k):
        return pltpu.make_async_remote_copy(
            hsend.at[other(y, k)], hbuf.at[y], sh.at[k], rh.at[y], device_id=(along_y(k), t), device_id_type=MESH
        )

    def hidden_in(k):
        peer = other(y, k)
        return pltpu.make_async_remote_copy(
            hsend.at[y], hbuf.at[peer], sh.at[k], rh.at[peer], device_id=(along_y(k), t), device_id_type=MESH
        )

    def source(there):
        return lax.rem(there, 4) * 2 + lax.div(there, 4)

    def codes_out(k):
        return pltpu.make_async_remote_copy(
            packed.at[lax.div(other(z, k), 4)], arrived.at[source(z)], s2.at[k], r2.at[source(z)],
            device_id=along_z(k), device_id_type=MESH,
        )

    def codes_in(k):
        place_in = source(other(z, k))
        return pltpu.make_async_remote_copy(
            packed.at[zh], arrived.at[place_in], s2.at[k], r2.at[place_in],
            device_id=along_z(k), device_id_type=MESH,
        )

    def place(j, c):
        return wbuf.at[pl.ds(pl.multiple_of(CHUNK * (2 * j + c), 16), CHUNK), :]

    def weight_copy(j, c):
        return pltpu.make_async_remote_copy(
            place(j, c), place(j, c), sf.at[j], rf.at[j], device_id=(sibling, t), device_id_type=MESH
        )

    def sum_out(k):
        return pltpu.make_async_remote_copy(
            pout.at[other(y, k)], pin.at[y], s3.at[k], r3.at[y], device_id=(along_y(k), t), device_id_type=MESH
        )

    def sum_in(k):
        peer = other(y, k)
        return pltpu.make_async_remote_copy(
            pout.at[y], pin.at[peer], s3.at[k], r3.at[peer], device_id=(along_y(k), t), device_id_type=MESH
        )

    pl.semaphore_wait(barrier, 18)
    for k in (2, 1, 3):
        for copy in to_x(k):
            copy.start()
    for k in FAR_FIRST:
        hidden_out(k).start()
    hbuf[y] = hsend[y]

    query_load.wait()
    swap = swap_matrix()
    flat = qbuf[...].astype(F32).reshape(FRESH, HEADS * HD)
    stacked = jnp.concatenate([flat[:, h * HD : (h + 1) * HD] for h in range(HEADS)], axis=0)
    qall[...] = dot(swap, stacked.astype(BF16))

    length_load.wait()
    lane = iota((ROWS, HD), 1)
    row = iota((ROWS, HD), 0)
    start = jnp.zeros((ROWS, HD), F32)
    for r in range(ROWS):
        start = jnp.where(row == r, lens[r].astype(F32), start)
    ladder = jnp.where(lane < HD // 2, lane, lane - HD // 2).astype(F32)
    freqs = jnp.exp(-math.log(1000000.0) * ladder / (HD // 2))
    for s in range(STEPS):
        angles = (start + float(s)) * freqs
        cosb[s * ROWS : (s + 1) * ROWS, :] = jnp.cos(angles)
        sine = jnp.sin(angles)
        sinb[s * ROWS : (s + 1) * ROWS, :] = jnp.where(lane < HD // 2, -sine, sine)

    key_load.wait()
    value_load.wait()
    scale = 1.0 / math.sqrt(HD)

    def attend(r, carry):
        rows = pl.ds(pl.multiple_of(r * QROWS, 8), QROWS)
        scores = dot_t(qall[rows, :].astype(BF16), kc[r]) * scale
        scores = jnp.where(iota((QROWS, CAP), 1) < lens[r], scores, -1e30)
        highest = jnp.max(scores, axis=-1, keepdims=True)
        weights = jnp.exp(scores - highest)
        mbuf[rows, :] = jnp.broadcast_to(highest, (QROWS, HD))
        lbuf[rows, :] = jnp.broadcast_to(jnp.sum(weights, axis=-1, keepdims=True), (QROWS, HD))
        acc[rows, :] = dot(weights.astype(BF16), vc[r])
        return carry

    lax.fori_loop(0, EARLY, attend, 0)

    i = iota((40, 64), 0)
    tens = lax.shift_right_logical(i * 205, 11)
    pick = jnp.where(iota((40, 64), 1) == i + 6 * tens, 1.0, 0.0).astype(BF16)
    i = iota((16, 128), 0)
    column = 4 * x + jnp.where(i < 8, i, i - 6)
    wanted = (iota((16, 128), 1) == column) & ((i < 2) | ((i >= 8) & (i < 10)))
    choose = jnp.where(wanted, 1.0, 0.0).astype(BF16)
    code_load.wait()
    scale_load.wait()
    for k in range(1, 4):
        for copy in from_x(k):
            copy.wait_recv()
    for k in range(4):
        inbox[k, 0:OWNED, 0 : 2 * WIDE] = boxc[k]
        inbox[k, 0:OWNED, 2 * WIDE : 2 * WIDE + 16] = boxs[k]
    got = inbox[...].reshape(64, 2 * WIDE + 128)
    factors = dot_t(choose, jnp.concatenate([got[:, 2 * WIDE :], jnp.zeros((64, 128), BF16)], axis=0))
    body = dot(pick, got[:, : 2 * WIDE])
    for half in range(2):
        last = jnp.concatenate([factors[8 * half : 8 * half + 8, :], jnp.zeros((8, 128), F32)], axis=1)
        whole = jnp.concatenate([body[:, half * WIDE : (half + 1) * WIDE], last], axis=0)
        packed[half] = whole.astype(BF16)
    for k in FAR_FIRST:
        codes_out(k).start()
    arrived[source(z)] = packed[zh]

    lax.fori_loop(EARLY, ROWS, attend, 0)

    for load in base_loads:
        load.wait()
    i = iota((CHUNK, 96), 0)
    tens = lax.shift_right_logical(i * 205, 11)
    odd = lax.rem(tens, 2)
    within = i - 10 * tens
    pair = lax.div(tens, 2)
    pick = jnp.where(iota((CHUNK, 96), 1) == odd * 48 + pair * 10 + within, 1.0, 0.0).astype(BF16)
    i = iota((CHUNK, 256), 0)
    tens = lax.shift_right_logical(i * 205, 11)
    odd = lax.rem(tens, 2)
    within = i - 10 * tens
    pair = lax.div(tens, 2)
    spread = jnp.where(iota((CHUNK, 256), 1) == odd * 128 + pair * 16 + within, 1.0, 0.0).astype(BF16)
    for k in range(1, 8):
        codes_in(k).wait_recv()
    for j in range(4):
        both = arrived[2 * j : 2 * j + 2].reshape(96, WIDE)
        update = dot(pick, both)
        columns = []
        for half in range(2):
            ends = arrived[2 * j + half, 32:48, 0:128].astype(F32)
            columns.append(
                jnp.concatenate(
                    [jnp.broadcast_to(ends[8 + part : 9 + part, :], (128, 128)) for part in range(2)], axis=0
                )
            )
        factor = dot_t(spread, jnp.concatenate(columns, axis=1).astype(BF16))
        place(j, core)[...] = (basebuf[j].astype(F32) + update * factor).astype(BF16)
        weight_copy(j, core).start()

    for k in range(1, 8):
        hidden_in(k).wait_recv()
    left = hbuf[...].astype(F32).reshape(8 * FRESH, SLICE).astype(BF16)
    gain_load.wait()
    for j in range(4):
        weight_copy(j, 1 - core).wait_recv()
    partial = dot(left, wbuf[...])
    pout[...] = partial.reshape(8, FRESH, WIDE)
    for k in FAR_FIRST:
        sum_out(k).start()
    pin[y] = pout[y]
    swap = swap_matrix()
    everything = qall[...].astype(BF16)
    shape = (ROWS, STEPS, HEADS, FRESH)
    col = iota(shape, 3)
    slot = jnp.where(col >= 2 * ROWS, 2, jnp.where(col >= ROWS, 1, 0))
    seen = (col - slot * ROWS == iota(shape, 0)) & (slot <= iota(shape, 1))
    bias = jnp.where(seen, 0.0, -1e30).astype(F32).reshape(ALLQ, FRESH)
    for k in range(1, 8):
        sum_in(k).wait_recv()
    projected = pin[0]
    for m in range(1, 8):
        projected = projected + pin[m]

    keys = projected[:, :HD]
    meansq = jnp.mean(keys * keys, axis=-1, keepdims=True)
    keys = keys * lax.rsqrt(meansq + 1e-06) * gain[...]
    turned = jnp.concatenate([keys[:, HD // 2 :], keys[:, : HD // 2]], axis=1)
    keys = (keys * cosb[...] + turned * sinb[...]).astype(BF16)
    values = projected[:, HD:].astype(BF16)

    scores = dot_t(everything, keys) * scale + bias
    before = mbuf[...]
    highest = jnp.maximum(before[:, :1], jnp.max(scores, axis=-1, keepdims=True))
    weights = jnp.exp(scores - highest)
    shrink = jnp.exp(before - highest)
    total = shrink * lbuf[...] + jnp.sum(weights, axis=-1, keepdims=True)
    result = (shrink * acc[...] + dot(weights.astype(BF16), values)) / total
    result = dot(swap, result.astype(BF16))
    result = jnp.concatenate([result[h * FRESH : (h + 1) * FRESH, :] for h in range(HEADS)], axis=1)
    out_ref[...] = result.reshape(STEPS, ROWS, HEADS * HD).astype(BF16)

    for k in range(1, 4):
        for copy in to_x(k):
            copy.wait_send()
    for j in range(4):
        weight_copy(j, core).wait_send()
    for k in range(1, 8):
        codes_out(k).wait_send()
        hidden_out(k).wait_send()
        sum_out(k).wait_send()


def per_device(hidden, queries, key_cache, value_cache, lengths, key_gain, base_weight, delta_codes, delta_scales):
    dma = pltpu.SemaphoreType.DMA
    return pl.pallas_call(
        kernel,
        out_shape=jax.ShapeDtypeStruct((STEPS, ROWS, HEADS * HD), BF16),
        in_specs=[pl.BlockSpec(memory_space=pl.ANY)] * 9,
        out_specs=pl.BlockSpec(memory_space=pltpu.VMEM),
        scratch_shapes=[
            pltpu.SMEM((ROWS,), jnp.int32),
            pltpu.VMEM((1, HD), F32),
            pltpu.VMEM((4, CHUNK, WIDE), BF16),
            pltpu.VMEM((STEPS, ROWS, HEADS * HD), BF16),
            pltpu.VMEM((STEPS, ROWS, D), BF16),
            pltpu.VMEM((ROWS, CAP, HD), BF16),
            pltpu.VMEM((ROWS, CAP, HD), BF16),
            pltpu.VMEM((4, OWNED, 2 * WIDE), BF16),
            pltpu.VMEM((4, OWNED, 16), BF16),
            pltpu.VMEM((4, 16, 2 * WIDE + 128), BF16),
            pltpu.VMEM((2, 48, WIDE), BF16),
            pltpu.VMEM((8, 48, WIDE), BF16),
            pltpu.VMEM((SLICE, WIDE), BF16),
            pltpu.VMEM((8, STEPS, ROWS, SLICE), BF16),
            pltpu.VMEM((8, STEPS, ROWS, SLICE), BF16),
            pltpu.VMEM((8, FRESH, WIDE), F32),
            pltpu.VMEM((8, FRESH, WIDE), F32),
            pltpu.VMEM((ALLQ, HD), F32),
            pltpu.VMEM((ALLQ, HD), F32),
            pltpu.VMEM((ALLQ, HD), F32),
            pltpu.VMEM((ALLQ, HD), F32),
            pltpu.VMEM((FRESH, HD), F32),
            pltpu.VMEM((FRESH, HD), F32),
            dma((8,)), dma((4,)),
            dma((4, 2)), dma((4, 2)),
            dma((8,)), dma((8,)),
            dma((8,)), dma((8,)),
            dma((4,)), dma((4,)),
            dma((8,)), dma((8,)),
        ],
        compiler_params=pltpu.CompilerParams(
            collective_id=0, has_side_effects=True, vmem_limit_bytes=56 * 1024 * 1024
        ),
        name="project_and_attend",
    )(
        lengths, key_gain.reshape(1, HD), delta_codes, delta_scales, base_weight, hidden, queries, key_cache, value_cache,
    )


def solution(mesh):
    return jax.shard_map(
        per_device,
        mesh=mesh,
        in_specs=(
            P(None, "group", None),
            P(None, "group", "tp"),
            P("group", None, "tp"),
            P("group", None, "tp"),
            P("group"),
            P(),
            P(None, "tp"),
            P(("group", "tp"), None),
            P(("group", "tp"), None),
        ),
        out_specs=P(None, "group", "tp"),
        check_vma=False,
    )
```

```python
import functools
import math

import jax
import jax.numpy as jnp
from jax import lax
from jax.experimental import pallas as pl
from jax.experimental.pallas import tpu as pltpu
from jax.sharding import PartitionSpec as P

MESH = pl.DeviceIdType.MESH
F32 = jnp.float32
BF16 = jnp.bfloat16

STEPS = 3
ROWS = 8
HD = 128
HEADS = 8
CAP = 512
D = 5120
OWNED = 10
CHUNK = 80
WIDE = 256
SLICE = D // 8
FAR_FIRST = (4, 3, 5, 2, 6, 1, 7)
QROWS = STEPS * HEADS
ALLQ = ROWS * QROWS
FRESH = STEPS * ROWS
EARLY = 3


def iota(shape, dim):
    return lax.broadcasted_iota(jnp.int32, shape, dim)


def dot(a, b):
    return jnp.dot(a, b, preferred_element_type=F32)


def dot_t(a, b):
    return lax.dot_general(a, b, (((1,), (1,)), ((), ())), preferred_element_type=F32)


def swap_matrix():
    shape = (8, STEPS, 8, ALLQ)
    hit = iota(shape, 3) == iota(shape, 2) * QROWS + iota(shape, 1) * 8 + iota(shape, 0)
    return jnp.where(hit, 1.0, 0.0).astype(F32).reshape(ALLQ, ALLQ).astype(BF16)


def kernel(
    lengths_hbm, gain_hbm, codes_hbm, scales_hbm, base_hbm, hidden_hbm, queries_hbm, kc_hbm, vc_hbm,
    out_ref,
    lens, gain, basebuf, qbuf, hfull, kc, vc,
    boxc, boxs, inbox, packed, arrived, wbuf, hsend, hbuf, left, pout, pin, qflat, qall, acc, mbuf, lbuf, cosb, sinb,
    local_sem, base_sem, s1, r1, sh, rh, s2, r2, sf, rf, s3, r3,
):
    g = lax.axis_index("group")
    t = lax.axis_index("tp")
    core = lax.rem(g, 2)
    y = lax.rem(lax.div(g, 2), 8)
    zl = lax.div(g, 16)
    x, zh = lax.div(t, 2), lax.rem(t, 2)
    z = zh * 4 + zl

    def peer_x(k):
        return lax.rem(x + k, 4)

    def along_y(k):
        return zl * 16 + other(y, k) * 2 + core

    def along_z(k):
        there = other(z, k)
        return lax.rem(there, 4) * 16 + y * 2 + core, x * 2 + lax.div(there, 4)

    sibling = g + 1 - 2 * core

    def other(mine, k):
        return lax.rem(mine + k, 8)

    loads = [
        pltpu.make_async_copy(src, dst, local_sem.at[i])
        for i, (src, dst) in enumerate(
            [
                (hidden_hbm, hfull),
                (codes_hbm.at[:, pl.ds(pl.multiple_of(x * 2 * WIDE, 128), 2 * WIDE)], boxc.at[x]),
                (scales_hbm, boxs.at[x]),
                (lengths_hbm, lens),
                (queries_hbm, qbuf),
                (gain_hbm, gain),
                (kc_hbm, kc),
                (vc_hbm, vc),
            ]
        )
    ]
    hidden_load, code_load, scale_load, length_load, query_load, gain_load, key_load, value_load = loads
    base_loads = [
        pltpu.make_async_copy(
            base_hbm.at[pl.ds(pl.multiple_of((16 * j + 2 * y + core) * CHUNK, 16), CHUNK), :],
            basebuf.at[j],
            base_sem.at[j],
        )
        for j in range(4)
    ]

    barrier = pltpu.get_barrier_semaphore()
    hidden_load.start()
    for k in range(1, 4):
        pl.semaphore_signal(barrier, inc=1, device_id=(g, peer_x(k) * 2 + zh), device_id_type=MESH)
    for k in FAR_FIRST:
        pl.semaphore_signal(barrier, inc=1, device_id=along_z(k), device_id_type=MESH)
    for k in FAR_FIRST:
        pl.semaphore_signal(barrier, inc=1, device_id=(along_y(k), t), device_id_type=MESH)
    pl.semaphore_signal(barrier, inc=1, device_id=(sibling, t), device_id_type=MESH)
    for load in loads[1:] + base_loads:
        load.start()

    inbox[...] = jnp.zeros(inbox.shape, BF16)
    hidden_load.wait()
    everything = hfull[...].astype(F32).reshape(FRESH, D)
    for m in range(8):
        for c in range(2):
            starts = [(16 * j + 2 * m + c) * CHUNK for j in range(4)]
            columns = jnp.concatenate([everything[:, a : a + CHUNK] for a in starts], axis=1)
            hsend[m, c] = columns.reshape(STEPS, ROWS, SLICE // 2).astype(BF16)

    def to_x(k):
        peer = peer_x(k)
        device = (g, peer * 2 + zh)
        return (
            pltpu.make_async_remote_copy(
                codes_hbm.at[:, pl.ds(pl.multiple_of(peer * 2 * WIDE, 128), 2 * WIDE)], boxc.at[x],
                s1.at[k, 0], r1.at[x, 0], device_id=device, device_id_type=MESH,
            ),
            pltpu.make_async_remote_copy(
                scales_hbm, boxs.at[x], s1.at[k, 1], r1.at[x, 1], device_id=device, device_id_type=MESH
            ),
        )

    def from_x(k):
        peer = peer_x(k)
        device = (g, peer * 2 + zh)
        return (
            pltpu.make_async_remote_copy(
                codes_hbm.at[:, pl.ds(pl.multiple_of(x * 2 * WIDE, 128), 2 * WIDE)], boxc.at[peer],
                s1.at[k, 0], r1.at[peer, 0], device_id=device, device_id_type=MESH,
            ),
            pltpu.make_async_remote_copy(
                scales_hbm, boxs.at[peer], s1.at[k, 1], r1.at[peer, 1], device_id=device, device_id_type=MESH
            ),
        )

    def hidden_out(k):
        return pltpu.make_async_remote_copy(
            hsend.at[other(y, k)], hbuf.at[y], sh.at[k], rh.at[y], device_id=(along_y(k), t), device_id_type=MESH
        )

    def hidden_in(k):
        peer = other(y, k)
        return pltpu.make_async_remote_copy(
            hsend.at[y], hbuf.at[peer], sh.at[k], rh.at[peer], device_id=(along_y(k), t), device_id_type=MESH
        )

    def source(there):
        return lax.rem(there, 4) * 2 + lax.div(there, 4)

    def codes_out(k):
        return pltpu.make_async_remote_copy(
            packed.at[lax.div(other(z, k), 4)], arrived.at[source(z)], s2.at[k], r2.at[source(z)],
            device_id=along_z(k), device_id_type=MESH,
        )

    def codes_in(k):
        place_in = source(other(z, k))
        return pltpu.make_async_remote_copy(
            packed.at[zh], arrived.at[place_in], s2.at[k], r2.at[place_in],
            device_id=along_z(k), device_id_type=MESH,
        )

    def weight_copy(c):
        return pltpu.make_async_remote_copy(
            wbuf.at[c], wbuf.at[c], sf, rf, device_id=(sibling, t), device_id_type=MESH
        )

    def sum_out(k):
        return pltpu.make_async_remote_copy(
            pout.at[other(y, k)], pin.at[y], s3.at[k], r3.at[y], device_id=(along_y(k), t), device_id_type=MESH
        )

    def sum_in(k):
        peer = other(y, k)
        return pltpu.make_async_remote_copy(
            pout.at[y], pin.at[peer], s3.at[k], r3.at[peer], device_id=(along_y(k), t), device_id_type=MESH
        )

    pl.semaphore_wait(barrier, 18)
    for k in (2, 1, 3):
        for copy in to_x(k):
            copy.start()
    for k in FAR_FIRST:
        hidden_out(k).start()
    hbuf[y] = hsend[y]

    query_load.wait()
    swap = swap_matrix()
    flat = qbuf[...].astype(F32).reshape(FRESH, HEADS * HD)
    stacked = jnp.concatenate([flat[:, h * HD : (h + 1) * HD] for h in range(HEADS)], axis=0)
    qflat[...] = stacked.astype(BF16)
    qall[...] = dot(swap, stacked.astype(BF16))

    length_load.wait()
    lane = iota((ROWS, HD), 1)
    row = iota((ROWS, HD), 0)
    start = jnp.zeros((ROWS, HD), F32)
    for r in range(ROWS):
        start = jnp.where(row == r, lens[r].astype(F32), start)
    ladder = jnp.where(lane < HD // 2, lane, lane - HD // 2).astype(F32)
    freqs = jnp.exp(-math.log(1000000.0) * ladder / (HD // 2))
    for s in range(STEPS):
        angles = (start + float(s)) * freqs
        cosb[s * ROWS : (s + 1) * ROWS, :] = jnp.cos(angles)
        sine = jnp.sin(angles)
        sinb[s * ROWS : (s + 1) * ROWS, :] = jnp.where(lane < HD // 2, -sine, sine)

    key_load.wait()
    value_load.wait()
    scale = 1.0 / math.sqrt(HD)

    def attend(r, carry):
        rows = pl.ds(pl.multiple_of(r * QROWS, 8), QROWS)
        scores = dot_t(qall[rows, :].astype(BF16), kc[r]) * scale
        scores = jnp.where(iota((QROWS, CAP), 1) < lens[r], scores, -1e30)
        highest = jnp.max(scores, axis=-1, keepdims=True)
        weights = jnp.exp(scores - highest)
        total = jnp.sum(weights, axis=-1, keepdims=True)
        mixed = dot(weights.astype(BF16), vc[r])
        for s in range(STEPS):
            there = pl.ds(s * ROWS + r, HEADS, stride=FRESH)
            these = slice(s * HEADS, (s + 1) * HEADS)
            mbuf[there, :] = jnp.broadcast_to(highest[these, :], (HEADS, HD))
            lbuf[there, :] = jnp.broadcast_to(total[these, :], (HEADS, HD))
            acc[there, :] = mixed[these, :]
        return carry

    lax.fori_loop(0, EARLY, attend, 0)

    i = iota((40, 64), 0)
    tens = lax.shift_right_logical(i * 205, 11)
    pick = jnp.where(iota((40, 64), 1) == i + 6 * tens, 1.0, 0.0).astype(BF16)
    i = iota((16, 128), 0)
    column = 4 * x + jnp.where(i < 8, i, i - 6)
    wanted = (iota((16, 128), 1) == column) & ((i < 2) | ((i >= 8) & (i < 10)))
    choose = jnp.where(wanted, 1.0, 0.0).astype(BF16)
    code_load.wait()
    scale_load.wait()
    for k in range(1, 4):
        for copy in from_x(k):
            copy.wait_recv()
    for k in range(4):
        inbox[k, 0:OWNED, 0 : 2 * WIDE] = boxc[k]
        inbox[k, 0:OWNED, 2 * WIDE : 2 * WIDE + 16] = boxs[k]
    got = inbox[...].reshape(64, 2 * WIDE + 128)
    factors = dot_t(choose, jnp.concatenate([got[:, 2 * WIDE :], jnp.zeros((64, 128), BF16)], axis=0))
    body = dot(pick, got[:, : 2 * WIDE])
    for half in range(2):
        last = jnp.concatenate([factors[8 * half : 8 * half + 8, :], jnp.zeros((8, 128), F32)], axis=1)
        whole = jnp.concatenate([body[:, half * WIDE : (half + 1) * WIDE], last], axis=0)
        packed[half] = whole.astype(BF16)
    for k in FAR_FIRST:
        codes_out(k).start()
    arrived[source(z)] = packed[zh]

    lax.fori_loop(EARLY, ROWS, attend, 0)

    for load in base_loads:
        load.wait()
    i = iota((CHUNK, 96), 0)
    tens = lax.shift_right_logical(i * 205, 11)
    odd = lax.rem(tens, 2)
    within = i - 10 * tens
    pair = lax.div(tens, 2)
    pick = jnp.where(iota((CHUNK, 96), 1) == odd * 48 + pair * 10 + within, 1.0, 0.0).astype(BF16)
    i = iota((CHUNK, 256), 0)
    tens = lax.shift_right_logical(i * 205, 11)
    odd = lax.rem(tens, 2)
    within = i - 10 * tens
    pair = lax.div(tens, 2)
    spread = jnp.where(iota((CHUNK, 256), 1) == odd * 128 + pair * 16 + within, 1.0, 0.0).astype(BF16)
    for k in range(1, 8):
        hidden_in(k).wait_recv()
    for c in range(2):
        left[c] = hbuf[:, c].astype(F32).reshape(8 * FRESH, SLICE // 2).astype(BF16)
    gain_load.wait()
    for k in range(1, 8):
        codes_in(k).wait_recv()
    sides, factors = [], []
    for j in range(4):
        sides.append(arrived[2 * j : 2 * j + 2].reshape(96, WIDE))
        columns = []
        for half in range(2):
            ends = arrived[2 * j + half, 32:48, 0:128].astype(F32)
            columns.append(
                jnp.concatenate(
                    [jnp.broadcast_to(ends[8 + part : 9 + part, :], (128, 128)) for part in range(2)], axis=0
                )
            )
        factors.append(jnp.concatenate(columns, axis=1).astype(BF16))
    update = dot(pick, jnp.concatenate(sides, axis=1))
    factor = dot_t(spread, jnp.concatenate(factors, axis=0))
    for j in range(4):
        part = slice(j * WIDE, (j + 1) * WIDE)
        wbuf[core, j * CHUNK : (j + 1) * CHUNK, :] = (
            basebuf[j].astype(F32) + update[:, part] * factor[:, part]
        ).astype(BF16)
    weight_copy(core).start()

    partial = dot(left[core], wbuf[core])
    weight_copy(1 - core).wait_recv()
    partial = partial + dot(left[1 - core], wbuf[1 - core])
    pout[...] = partial.reshape(8, FRESH, WIDE)
    for k in FAR_FIRST:
        sum_out(k).start()
    pin[y] = pout[y]
    everything = qflat[...]
    shape = (HEADS, STEPS, ROWS, FRESH)
    col = iota(shape, 3)
    slot = jnp.where(col >= 2 * ROWS, 2, jnp.where(col >= ROWS, 1, 0))
    seen = (col - slot * ROWS == iota(shape, 2)) & (slot <= iota(shape, 1))
    bias = jnp.where(seen, 0.0, -1e30).astype(F32).reshape(ALLQ, FRESH)
    for k in range(1, 4):
        for copy in to_x(k):
            copy.wait_send()
    for k in FAR_FIRST:
        hidden_out(k).wait_send()
        codes_out(k).wait_send()
    weight_copy(core).wait_send()
    for k in range(1, 8):
        sum_in(k).wait_recv()
    projected = pin[0]
    for m in range(1, 8):
        projected = projected + pin[m]

    keys = projected[:, :HD]
    meansq = jnp.mean(keys * keys, axis=-1, keepdims=True)
    keys = keys * lax.rsqrt(meansq + 1e-06) * gain[...]
    turned = jnp.concatenate([keys[:, HD // 2 :], keys[:, : HD // 2]], axis=1)
    keys = (keys * cosb[...] + turned * sinb[...]).astype(BF16)
    values = projected[:, HD:].astype(BF16)

    scores = dot_t(everything, keys) * scale + bias
    before = mbuf[...]
    highest = jnp.maximum(before[:, :1], jnp.max(scores, axis=-1, keepdims=True))
    weights = jnp.exp(scores - highest)
    shrink = jnp.exp(before - highest)
    total = shrink * lbuf[...] + jnp.sum(weights, axis=-1, keepdims=True)
    result = (shrink * acc[...] + dot(weights.astype(BF16), values)) / total
    result = jnp.concatenate([result[h * FRESH : (h + 1) * FRESH, :] for h in range(HEADS)], axis=1)
    out_ref[...] = result.reshape(STEPS, ROWS, HEADS * HD).astype(BF16)

    for k in FAR_FIRST:
        sum_out(k).wait_send()


def per_device(hidden, queries, key_cache, value_cache, lengths, key_gain, base_weight, delta_codes, delta_scales):
    dma = pltpu.SemaphoreType.DMA
    return pl.pallas_call(
        kernel,
        out_shape=pltpu.VMEM((STEPS, ROWS, HEADS * HD), BF16),
        in_specs=[pl.BlockSpec(memory_space=pl.ANY)] * 9,
        out_specs=pl.BlockSpec(memory_space=pltpu.VMEM),
        scratch_shapes=[
            pltpu.SMEM((ROWS,), jnp.int32),
            pltpu.VMEM((1, HD), F32),
            pltpu.VMEM((4, CHUNK, WIDE), BF16),
            pltpu.VMEM((STEPS, ROWS, HEADS * HD), BF16),
            pltpu.VMEM((STEPS, ROWS, D), BF16),
            pltpu.VMEM((ROWS, CAP, HD), BF16),
            pltpu.VMEM((ROWS, CAP, HD), BF16),
            pltpu.VMEM((4, OWNED, 2 * WIDE), BF16),
            pltpu.VMEM((4, OWNED, 16), BF16),
            pltpu.VMEM((4, 16, 2 * WIDE + 128), BF16),
            pltpu.VMEM((2, 48, WIDE), BF16),
            pltpu.VMEM((8, 48, WIDE), BF16),
            pltpu.VMEM((2, SLICE // 2, WIDE), BF16),
            pltpu.VMEM((8, 2, STEPS, ROWS, SLICE // 2), BF16),
            pltpu.VMEM((8, 2, STEPS, ROWS, SLICE // 2), BF16),
            pltpu.VMEM((2, 8 * FRESH, SLICE // 2), BF16),
            pltpu.VMEM((8, FRESH, WIDE), F32),
            pltpu.VMEM((8, FRESH, WIDE), F32),
            pltpu.VMEM((ALLQ, HD), BF16),
            pltpu.VMEM((ALLQ, HD), F32),
            pltpu.VMEM((ALLQ, HD), F32),
            pltpu.VMEM((ALLQ, HD), F32),
            pltpu.VMEM((ALLQ, HD), F32),
            pltpu.VMEM((FRESH, HD), F32),
            pltpu.VMEM((FRESH, HD), F32),
            dma((8,)), dma((4,)),
            dma((4, 2)), dma((4, 2)),
            dma((8,)), dma((8,)),
            dma((8,)), dma((8,)),
            dma, dma,
            dma((8,)), dma((8,)),
        ],
        compiler_params=pltpu.CompilerParams(
            collective_id=0, has_side_effects=True, vmem_limit_bytes=56 * 1024 * 1024
        ),
        name="project_and_attend",
    )(
        lengths, key_gain.reshape(1, HD), delta_codes, delta_scales, base_weight, hidden, queries, key_cache, value_cache,
    )


def solution(mesh):
    return jax.shard_map(
        per_device,
        mesh=mesh,
        in_specs=(
            P(None, "group", None),
            P(None, "group", "tp"),
            P("group", None, "tp"),
            P("group", None, "tp"),
            P("group"),
            P(),
            P(None, "tp"),
            P(("group", "tp"), None),
            P(("group", "tp"), None),
        ),
        out_specs=P(None, "group", "tp"),
        check_vma=False,
    )
```

```python
import functools
import math

import jax
import jax.numpy as jnp
from jax import lax
from jax.experimental import pallas as pl
from jax.experimental.pallas import tpu as pltpu
from jax.sharding import PartitionSpec as P

MESH = pl.DeviceIdType.MESH
F32 = jnp.float32
BF16 = jnp.bfloat16

STEPS = 3
ROWS = 8
HD = 128
HEADS = 8
CAP = 512
D = 5120
OWNED = 10
CHUNK = 80
WIDE = 256
SLICE = D // 8
FAR_FIRST = (4, 3, 5, 2, 6, 1, 7)
Y_ORDER = (0, 1, 2, 3, 7, 6, 5, 4)
QROWS = STEPS * HEADS
ALLQ = ROWS * QROWS
FRESH = STEPS * ROWS
EARLY = 0


def iota(shape, dim):
    return lax.broadcasted_iota(jnp.int32, shape, dim)


def dot(a, b):
    return jnp.dot(a, b, preferred_element_type=F32)


def dot_t(a, b):
    return lax.dot_general(a, b, (((1,), (1,)), ((), ())), preferred_element_type=F32)


def swap_matrix():
    shape = (8, STEPS, 8, ALLQ)
    hit = iota(shape, 3) == iota(shape, 2) * QROWS + iota(shape, 1) * 8 + iota(shape, 0)
    return jnp.where(hit, 1.0, 0.0).astype(F32).reshape(ALLQ, ALLQ).astype(BF16)


def kernel(
    lengths_hbm, gain_hbm, codes_hbm, scales_hbm, base_hbm, hidden_hbm, queries_hbm, kc_hbm, vc_hbm,
    out_ref,
    lens, gain, basebuf, qbuf, hfull, kc, vc,
    boxc, boxs, inbox, packed, arrived, wbuf, hsend, hbuf, left, pout, pin, qflat, qall, acc, mbuf, lbuf, cosb, sinb,
    local_sem, base_sem, s1, r1, sh, rh, s2, r2, sf, rf, s3, r3, ready_y, ready_z,
):
    g = lax.axis_index("group")
    t = lax.axis_index("tp")
    core = lax.rem(g, 2)
    y = lax.rem(lax.div(g, 2), 8)
    zl = lax.div(g, 16)
    x, zh = lax.div(t, 2), lax.rem(t, 2)
    z = zh * 4 + zl

    def peer_x(k):
        return lax.rem(x + k, 4)

    def along_y(k):
        return zl * 16 + other(y, k) * 2 + core

    def along_z(k):
        there = other(z, k)
        return lax.rem(there, 4) * 16 + y * 2 + core, x * 2 + lax.div(there, 4)

    sibling = g + 1 - 2 * core

    def other(mine, k):
        return lax.rem(mine + k, 8)

    loads = [
        pltpu.make_async_copy(src, dst, local_sem.at[i])
        for i, (src, dst) in enumerate(
            [
                (hidden_hbm, hfull),
                (codes_hbm.at[:, pl.ds(pl.multiple_of(x * 2 * WIDE, 128), 2 * WIDE)], boxc.at[x]),
                (scales_hbm, boxs.at[x]),
                (lengths_hbm, lens),
                (queries_hbm, qbuf),
                (gain_hbm, gain),
                (kc_hbm, kc),
                (vc_hbm, vc),
            ]
        )
    ]
    hidden_load, code_load, scale_load, length_load, query_load, gain_load, key_load, value_load = loads
    base_loads = [
        pltpu.make_async_copy(
            base_hbm.at[pl.ds(pl.multiple_of((16 * j + 2 * y + core) * CHUNK, 16), CHUNK), :],
            basebuf.at[j],
            base_sem.at[j],
        )
        for j in range(4)
    ]

    def to_x(k):
        peer = peer_x(k)
        device = (g, peer * 2 + zh)
        return (
            pltpu.make_async_remote_copy(
                codes_hbm.at[:, pl.ds(pl.multiple_of(peer * 2 * WIDE, 128), 2 * WIDE)], boxc.at[x],
                s1.at[k, 0], r1.at[x, 0], device_id=device, device_id_type=MESH,
            ),
            pltpu.make_async_remote_copy(
                scales_hbm, boxs.at[x], s1.at[k, 1], r1.at[x, 1], device_id=device, device_id_type=MESH
            ),
        )

    def from_x(k):
        peer = peer_x(k)
        device = (g, peer * 2 + zh)
        return (
            pltpu.make_async_remote_copy(
                codes_hbm.at[:, pl.ds(pl.multiple_of(x * 2 * WIDE, 128), 2 * WIDE)], boxc.at[peer],
                s1.at[k, 0], r1.at[peer, 0], device_id=device, device_id_type=MESH,
            ),
            pltpu.make_async_remote_copy(
                scales_hbm, boxs.at[peer], s1.at[k, 1], r1.at[peer, 1], device_id=device, device_id_type=MESH
            ),
        )

    def hidden_out(k):
        return pltpu.make_async_remote_copy(
            hsend.at[other(y, k)], hbuf.at[y], sh.at[k], rh.at[y], device_id=(along_y(k), t), device_id_type=MESH
        )

    def hidden_in(k):
        peer = other(y, k)
        return pltpu.make_async_remote_copy(
            hsend.at[y], hbuf.at[peer], sh.at[k], rh.at[peer], device_id=(along_y(k), t), device_id_type=MESH
        )

    def source(there):
        return lax.rem(there, 4) * 2 + lax.div(there, 4)

    def codes_out(k):
        return pltpu.make_async_remote_copy(
            packed.at[lax.div(other(z, k), 4)], arrived.at[source(z)], s2.at[k], r2.at[source(z)],
            device_id=along_z(k), device_id_type=MESH,
        )

    def codes_in(k):
        place_in = source(other(z, k))
        return pltpu.make_async_remote_copy(
            packed.at[zh], arrived.at[place_in], s2.at[k], r2.at[place_in],
            device_id=along_z(k), device_id_type=MESH,
        )

    def weight_copy(c):
        return pltpu.make_async_remote_copy(
            wbuf.at[c], wbuf.at[c], sf, rf, device_id=(sibling, t), device_id_type=MESH
        )

    def sum_out(k):
        return pltpu.make_async_remote_copy(
            pout.at[other(y, k)], pin.at[y], s3.at[k], r3.at[y], device_id=(along_y(k), t), device_id_type=MESH
        )

    def sum_in(k):
        peer = other(y, k)
        return pltpu.make_async_remote_copy(
            pout.at[y], pin.at[peer], s3.at[k], r3.at[peer], device_id=(along_y(k), t), device_id_type=MESH
        )

    barrier = pltpu.get_barrier_semaphore()
    half_y = lax.div(y, 4)
    rank = y + half_y * (11 - 2 * y)
    y_devices = [(zl * 16 + there * 2 + core, t) for there in Y_ORDER]
    z_devices = [((there % 4) * 16 + y * 2 + core, x * 2 + there // 4) for there in range(8)]

    for k in (2, 1, 3):
        pl.semaphore_signal(barrier, inc=1, device_id=(g, peer_x(k) * 2 + zh), device_id_type=MESH)
    pl.semaphore_signal(barrier, inc=1, device_id=(sibling, t), device_id_type=MESH)
    hidden_load.start()
    for n in range(1, 8):

        @pl.when(z < n)
        def _(n=n):
            pl.semaphore_signal(barrier, inc=1, device_id=z_devices[n], device_id_type=MESH)

        @pl.when(rank < n)
        def _(n=n):
            pl.semaphore_signal(barrier, inc=1, device_id=y_devices[n], device_id_type=MESH)

    pl.semaphore_wait(barrier, 4 + z + rank)
    for k in (2, 1, 3):
        for copy in to_x(k):
            copy.start()
    for n in range(7):

        @pl.when(z > n)
        def _(n=n):
            pl.semaphore_signal(ready_z, inc=1, device_id=z_devices[n], device_id_type=MESH)

        @pl.when(rank > n)
        def _(n=n):
            pl.semaphore_signal(ready_y, inc=1, device_id=y_devices[n], device_id_type=MESH)

    for load in loads[1:] + base_loads:
        load.start()
    inbox[...] = jnp.zeros(inbox.shape, BF16)

    hidden_load.wait()
    everything = hfull[...].astype(F32).reshape(FRESH, D)
    for m in range(8):
        for c in range(2):
            starts = [(16 * j + 2 * m + c) * CHUNK for j in range(4)]
            columns = jnp.concatenate([everything[:, a : a + CHUNK] for a in starts], axis=1)
            hsend[m, c] = columns.reshape(STEPS, ROWS, SLICE // 2).astype(BF16)

    hbuf[y] = hsend[y]

    @pl.when(rank < 7)
    def _():
        pl.semaphore_wait(ready_y, 7 - rank)

    for k in FAR_FIRST:
        hidden_out(k).start()
    query_load.wait()
    swap = swap_matrix()
    flat = qbuf[...].astype(F32).reshape(FRESH, HEADS * HD)
    stacked = jnp.concatenate([flat[:, h * HD : (h + 1) * HD] for h in range(HEADS)], axis=0)
    qflat[...] = stacked.astype(BF16)
    qall[...] = dot(swap, stacked.astype(BF16))

    length_load.wait()
    lane = iota((ROWS, HD), 1)
    row = iota((ROWS, HD), 0)
    start = jnp.zeros((ROWS, HD), F32)
    for r in range(ROWS):
        start = jnp.where(row == r, lens[r].astype(F32), start)
    ladder = jnp.where(lane < HD // 2, lane, lane - HD // 2).astype(F32)
    freqs = jnp.exp(-math.log(1000000.0) * ladder / (HD // 2))
    for s in range(STEPS):
        angles = (start + float(s)) * freqs
        cosb[s * ROWS : (s + 1) * ROWS, :] = jnp.cos(angles)
        sine = jnp.sin(angles)
        sinb[s * ROWS : (s + 1) * ROWS, :] = jnp.where(lane < HD // 2, -sine, sine)

    key_load.wait()
    value_load.wait()
    scale = 1.0 / math.sqrt(HD)

    def attend(r, carry):
        rows = pl.ds(pl.multiple_of(r * QROWS, 8), QROWS)
        scores = dot_t(qall[rows, :].astype(BF16), kc[r]) * scale
        scores = jnp.where(iota((QROWS, CAP), 1) < lens[r], scores, -1e30)
        highest = jnp.max(scores, axis=-1, keepdims=True)
        weights = jnp.exp(scores - highest)
        total = jnp.sum(weights, axis=-1, keepdims=True)
        mixed = dot(weights.astype(BF16), vc[r])
        for s in range(STEPS):
            there = pl.ds(s * ROWS + r, HEADS, stride=FRESH)
            these = slice(s * HEADS, (s + 1) * HEADS)
            mbuf[there, :] = jnp.broadcast_to(highest[these, :], (HEADS, HD))
            lbuf[there, :] = jnp.broadcast_to(total[these, :], (HEADS, HD))
            acc[there, :] = mixed[these, :]
        return carry

    lax.fori_loop(0, EARLY, attend, 0)


    i = iota((40, 64), 0)
    tens = lax.shift_right_logical(i * 205, 11)
    pick = jnp.where(iota((40, 64), 1) == i + 6 * tens, 1.0, 0.0).astype(BF16)
    i = iota((16, 128), 0)
    column = 4 * x + jnp.where(i < 8, i, i - 6)
    wanted = (iota((16, 128), 1) == column) & ((i < 2) | ((i >= 8) & (i < 10)))
    choose = jnp.where(wanted, 1.0, 0.0).astype(BF16)
    code_load.wait()
    scale_load.wait()
    for k in range(1, 4):
        for copy in from_x(k):
            copy.wait_recv()
    for k in range(4):
        inbox[k, 0:OWNED, 0 : 2 * WIDE] = boxc[k]
        inbox[k, 0:OWNED, 2 * WIDE : 2 * WIDE + 16] = boxs[k]
    got = inbox[...].reshape(64, 2 * WIDE + 128)
    factors = dot_t(choose, jnp.concatenate([got[:, 2 * WIDE :], jnp.zeros((64, 128), BF16)], axis=0))
    body = dot(pick, got[:, : 2 * WIDE])
    for half in range(2):
        last = jnp.concatenate([factors[8 * half : 8 * half + 8, :], jnp.zeros((8, 128), F32)], axis=1)
        whole = jnp.concatenate([body[:, half * WIDE : (half + 1) * WIDE], last], axis=0)
        packed[half] = whole.astype(BF16)
    @pl.when(z < 7)
    def _():
        pl.semaphore_wait(ready_z, 7 - z)

    for k in FAR_FIRST:
        codes_out(k).start()
    arrived[source(z)] = packed[zh]

    lax.fori_loop(EARLY, ROWS, attend, 0)

    for load in base_loads:
        load.wait()
    i = iota((CHUNK, 96), 0)
    tens = lax.shift_right_logical(i * 205, 11)
    odd = lax.rem(tens, 2)
    within = i - 10 * tens
    pair = lax.div(tens, 2)
    pick = jnp.where(iota((CHUNK, 96), 1) == odd * 48 + pair * 10 + within, 1.0, 0.0).astype(BF16)
    i = iota((CHUNK, 256), 0)
    tens = lax.shift_right_logical(i * 205, 11)
    odd = lax.rem(tens, 2)
    within = i - 10 * tens
    pair = lax.div(tens, 2)
    spread = jnp.where(iota((CHUNK, 256), 1) == odd * 128 + pair * 16 + within, 1.0, 0.0).astype(BF16)
    for k in range(1, 8):
        hidden_in(k).wait_recv()
    for c in range(2):
        left[c] = hbuf[:, c].astype(F32).reshape(8 * FRESH, SLICE // 2).astype(BF16)
    gain_load.wait()
    for k in range(1, 8):
        codes_in(k).wait_recv()
    sides, factors = [], []
    for j in range(4):
        sides.append(arrived[2 * j : 2 * j + 2].reshape(96, WIDE))
        columns = []
        for half in range(2):
            ends = arrived[2 * j + half, 32:48, 0:128].astype(F32)
            columns.append(
                jnp.concatenate(
                    [jnp.broadcast_to(ends[8 + part : 9 + part, :], (128, 128)) for part in range(2)], axis=0
                )
            )
        factors.append(jnp.concatenate(columns, axis=1).astype(BF16))
    update = dot(pick, jnp.concatenate(sides, axis=1))
    factor = dot_t(spread, jnp.concatenate(factors, axis=0))
    for j in range(4):
        part = slice(j * WIDE, (j + 1) * WIDE)
        wbuf[core, j * CHUNK : (j + 1) * CHUNK, :] = (
            basebuf[j].astype(F32) + update[:, part] * factor[:, part]
        ).astype(BF16)
    weight_copy(core).start()

    partial = dot(left[core], wbuf[core])
    weight_copy(1 - core).wait_recv()
    partial = partial + dot(left[1 - core], wbuf[1 - core])
    pout[...] = partial.reshape(8, FRESH, WIDE)
    for k in FAR_FIRST:
        sum_out(k).start()
    pin[y] = pout[y]
    everything = qflat[...]
    shape = (HEADS, STEPS, ROWS, FRESH)
    col = iota(shape, 3)
    slot = jnp.where(col >= 2 * ROWS, 2, jnp.where(col >= ROWS, 1, 0))
    seen = (col - slot * ROWS == iota(shape, 2)) & (slot <= iota(shape, 1))
    bias = jnp.where(seen, 0.0, -1e30).astype(F32).reshape(ALLQ, FRESH)
    for k in range(1, 4):
        for copy in to_x(k):
            copy.wait_send()
    for k in FAR_FIRST:
        hidden_out(k).wait_send()
        codes_out(k).wait_send()
    weight_copy(core).wait_send()
    for k in range(1, 8):
        sum_in(k).wait_recv()
    projected = pin[0]
    for m in range(1, 8):
        projected = projected + pin[m]

    keys = projected[:, :HD]
    meansq = jnp.mean(keys * keys, axis=-1, keepdims=True)
    keys = keys * lax.rsqrt(meansq + 1e-06) * gain[...]
    turned = jnp.concatenate([keys[:, HD // 2 :], keys[:, : HD // 2]], axis=1)
    keys = (keys * cosb[...] + turned * sinb[...]).astype(BF16)
    values = projected[:, HD:].astype(BF16)

    scores = dot_t(everything, keys) * scale + bias
    before = mbuf[...]
    highest = jnp.maximum(before[:, :1], jnp.max(scores, axis=-1, keepdims=True))
    weights = jnp.exp(scores - highest)
    shrink = jnp.exp(before - highest)
    total = shrink * lbuf[...] + jnp.sum(weights, axis=-1, keepdims=True)
    result = (shrink * acc[...] + dot(weights.astype(BF16), values)) / total
    result = jnp.concatenate([result[h * FRESH : (h + 1) * FRESH, :] for h in range(HEADS)], axis=1)
    out_ref[...] = result.reshape(STEPS, ROWS, HEADS * HD).astype(BF16)

    for k in FAR_FIRST:
        sum_out(k).wait_send()


def per_device(hidden, queries, key_cache, value_cache, lengths, key_gain, base_weight, delta_codes, delta_scales):
    dma = pltpu.SemaphoreType.DMA
    return pl.pallas_call(
        kernel,
        out_shape=pltpu.VMEM((STEPS, ROWS, HEADS * HD), BF16),
        in_specs=[pl.BlockSpec(memory_space=pl.ANY)] * 9,
        out_specs=pl.BlockSpec(memory_space=pltpu.VMEM),
        scratch_shapes=[
            pltpu.SMEM((ROWS,), jnp.int32),
            pltpu.VMEM((1, HD), F32),
            pltpu.VMEM((4, CHUNK, WIDE), BF16),
            pltpu.VMEM((STEPS, ROWS, HEADS * HD), BF16),
            pltpu.VMEM((STEPS, ROWS, D), BF16),
            pltpu.VMEM((ROWS, CAP, HD), BF16),
            pltpu.VMEM((ROWS, CAP, HD), BF16),
            pltpu.VMEM((4, OWNED, 2 * WIDE), BF16),
            pltpu.VMEM((4, OWNED, 16), BF16),
            pltpu.VMEM((4, 16, 2 * WIDE + 128), BF16),
            pltpu.VMEM((2, 48, WIDE), BF16),
            pltpu.VMEM((8, 48, WIDE), BF16),
            pltpu.VMEM((2, SLICE // 2, WIDE), BF16),
            pltpu.VMEM((8, 2, STEPS, ROWS, SLICE // 2), BF16),
            pltpu.VMEM((8, 2, STEPS, ROWS, SLICE // 2), BF16),
            pltpu.VMEM((2, 8 * FRESH, SLICE // 2), BF16),
            pltpu.VMEM((8, FRESH, WIDE), F32),
            pltpu.VMEM((8, FRESH, WIDE), F32),
            pltpu.VMEM((ALLQ, HD), BF16),
            pltpu.VMEM((ALLQ, HD), F32),
            pltpu.VMEM((ALLQ, HD), F32),
            pltpu.VMEM((ALLQ, HD), F32),
            pltpu.VMEM((ALLQ, HD), F32),
            pltpu.VMEM((FRESH, HD), F32),
            pltpu.VMEM((FRESH, HD), F32),
            dma((8,)), dma((4,)),
            dma((4, 2)), dma((4, 2)),
            dma((8,)), dma((8,)),
            dma((8,)), dma((8,)),
            dma, dma,
            dma((8,)), dma((8,)),
            pltpu.SemaphoreType.REGULAR, pltpu.SemaphoreType.REGULAR,
        ],
        compiler_params=pltpu.CompilerParams(
            collective_id=0, has_side_effects=True, vmem_limit_bytes=56 * 1024 * 1024
        ),
        name="project_and_attend",
    )(
        lengths, key_gain.reshape(1, HD), delta_codes, delta_scales, base_weight, hidden, queries, key_cache, value_cache,
    )


def solution(mesh):
    return jax.shard_map(
        per_device,
        mesh=mesh,
        in_specs=(
            P(None, "group", None),
            P(None, "group", "tp"),
            P("group", None, "tp"),
            P("group", None, "tp"),
            P("group"),
            P(),
            P(None, "tp"),
            P(("group", "tp"), None),
            P(("group", "tp"), None),
        ),
        out_specs=P(None, "group", "tp"),
        check_vma=False,
    )
```

```python
import functools
import math

import jax
import jax.numpy as jnp
from jax import lax
from jax.experimental import pallas as pl
from jax.experimental.pallas import tpu as pltpu
from jax.sharding import PartitionSpec as P

MESH = pl.DeviceIdType.MESH
F32 = jnp.float32
BF16 = jnp.bfloat16

STEPS = 3
ROWS = 8
HD = 128
HEADS = 8
CAP = 512
D = 5120
OWNED = 10
CHUNK = 80
WIDE = 256
SLICE = D // 8
FAR_FIRST = (4, 3, 5, 2, 6, 1, 7)
Y_ORDER = (0, 1, 2, 3, 7, 6, 5, 4)
QROWS = STEPS * HEADS
ALLQ = ROWS * QROWS
FRESH = STEPS * ROWS
EARLY = 0


def iota(shape, dim):
    return lax.broadcasted_iota(jnp.int32, shape, dim)


def dot(a, b):
    return jnp.dot(a, b, preferred_element_type=F32)


def dot_t(a, b):
    return lax.dot_general(a, b, (((1,), (1,)), ((), ())), preferred_element_type=F32)


def swap_matrix():
    shape = (8, STEPS, 8, ALLQ)
    hit = iota(shape, 3) == iota(shape, 2) * QROWS + iota(shape, 1) * 8 + iota(shape, 0)
    return jnp.where(hit, 1.0, 0.0).astype(F32).reshape(ALLQ, ALLQ).astype(BF16)


def kernel(
    lengths_hbm, gain_hbm, codes_hbm, scales_hbm, base_hbm, hidden_hbm, queries_hbm, kc_hbm, vc_hbm,
    out_ref,
    lens, gain, basebuf, qbuf, hfull, kc, vc,
    boxc, boxs, inbox, packed, arrived, wbuf, hsend, hbuf, left, pout, pin, qflat, qall, acc, mbuf, lbuf, cosb, sinb,
    local_sem, base_sem, s1, r1, sh, rh, s2, r2, sf, rf, s3, r3, ready_y, ready_z, ready_far,
):
    g = lax.axis_index("group")
    t = lax.axis_index("tp")
    core = lax.rem(g, 2)
    y = lax.rem(lax.div(g, 2), 8)
    zl = lax.div(g, 16)
    x, zh = lax.div(t, 2), lax.rem(t, 2)
    z = zh * 4 + zl

    def peer_x(k):
        return lax.rem(x + k, 4)

    def along_y(k):
        return zl * 16 + other(y, k) * 2 + core

    def along_z(k):
        there = other(z, k)
        return lax.rem(there, 4) * 16 + y * 2 + core, x * 2 + lax.div(there, 4)

    sibling = g + 1 - 2 * core

    def other(mine, k):
        return lax.rem(mine + k, 8)

    loads = [
        pltpu.make_async_copy(src, dst, local_sem.at[i])
        for i, (src, dst) in enumerate(
            [
                (hidden_hbm, hfull),
                (codes_hbm.at[:, pl.ds(pl.multiple_of(x * 2 * WIDE, 128), 2 * WIDE)], boxc.at[x]),
                (scales_hbm, boxs.at[x]),
                (lengths_hbm, lens),
                (queries_hbm, qbuf),
                (gain_hbm, gain),
                (kc_hbm, kc),
                (vc_hbm, vc),
            ]
        )
    ]
    hidden_load, code_load, scale_load, length_load, query_load, gain_load, key_load, value_load = loads
    base_loads = [
        pltpu.make_async_copy(
            base_hbm.at[pl.ds(pl.multiple_of((16 * j + 2 * y + core) * CHUNK, 16), CHUNK), :],
            basebuf.at[j],
            base_sem.at[j],
        )
        for j in range(4)
    ]

    def to_x(k):
        peer = peer_x(k)
        device = (g, peer * 2 + zh)
        return (
            pltpu.make_async_remote_copy(
                codes_hbm.at[:, pl.ds(pl.multiple_of(peer * 2 * WIDE, 128), 2 * WIDE)], boxc.at[x],
                s1.at[k, 0], r1.at[x, 0], device_id=device, device_id_type=MESH,
            ),
            pltpu.make_async_remote_copy(
                scales_hbm, boxs.at[x], s1.at[k, 1], r1.at[x, 1], device_id=device, device_id_type=MESH
            ),
        )

    def from_x(k):
        peer = peer_x(k)
        device = (g, peer * 2 + zh)
        return (
            pltpu.make_async_remote_copy(
                codes_hbm.at[:, pl.ds(pl.multiple_of(x * 2 * WIDE, 128), 2 * WIDE)], boxc.at[peer],
                s1.at[k, 0], r1.at[peer, 0], device_id=device, device_id_type=MESH,
            ),
            pltpu.make_async_remote_copy(
                scales_hbm, boxs.at[peer], s1.at[k, 1], r1.at[peer, 1], device_id=device, device_id_type=MESH
            ),
        )

    def hidden_out(k):
        return pltpu.make_async_remote_copy(
            hsend.at[other(y, k)], hbuf.at[y], sh.at[k], rh.at[y], device_id=(along_y(k), t), device_id_type=MESH
        )

    def hidden_in(k):
        peer = other(y, k)
        return pltpu.make_async_remote_copy(
            hsend.at[y], hbuf.at[peer], sh.at[k], rh.at[peer], device_id=(along_y(k), t), device_id_type=MESH
        )

    def source(there):
        return lax.rem(there, 4) * 2 + lax.div(there, 4)

    def codes_out(n):
        return pltpu.make_async_remote_copy(
            packed.at[n // 4], arrived.at[source(z)], s2.at[n], r2.at[source(z)],
            device_id=z_devices[n], device_id_type=MESH,
        )

    def codes_in(k):
        place_in = source(other(z, k))
        return pltpu.make_async_remote_copy(
            packed.at[zh], arrived.at[place_in], s2.at[k], r2.at[place_in],
            device_id=along_z(k), device_id_type=MESH,
        )

    def weight_copy(c):
        return pltpu.make_async_remote_copy(
            wbuf.at[c], wbuf.at[c], sf, rf, device_id=(sibling, t), device_id_type=MESH
        )

    def sum_out(k):
        return pltpu.make_async_remote_copy(
            pout.at[other(y, k)], pin.at[y], s3.at[k], r3.at[y], device_id=(along_y(k), t), device_id_type=MESH
        )

    def sum_in(k):
        peer = other(y, k)
        return pltpu.make_async_remote_copy(
            pout.at[y], pin.at[peer], s3.at[k], r3.at[peer], device_id=(along_y(k), t), device_id_type=MESH
        )

    barrier = pltpu.get_barrier_semaphore()
    half_y = lax.div(y, 4)
    rank = y + half_y * (11 - 2 * y)
    y_devices = [(zl * 16 + there * 2 + core, t) for there in Y_ORDER]
    z_devices = [((there % 4) * 16 + y * 2 + core, x * 2 + there // 4) for there in range(8)]

    for k in (2, 1, 3):
        pl.semaphore_signal(barrier, inc=1, device_id=(g, peer_x(k) * 2 + zh), device_id_type=MESH)
    pl.semaphore_signal(barrier, inc=1, device_id=(sibling, t), device_id_type=MESH)
    hidden_load.start()
    for n in range(1, 8):

        @pl.when(z < n)
        def _(n=n):
            pl.semaphore_signal(barrier, inc=1, device_id=z_devices[n], device_id_type=MESH)

        @pl.when(rank < n)
        def _(n=n):
            pl.semaphore_signal(barrier, inc=1, device_id=y_devices[n], device_id_type=MESH)

    pl.semaphore_wait(barrier, 4 + z + rank)
    for k in (2, 1, 3):
        for copy in to_x(k):
            copy.start()
    for n in range(7):

        @pl.when((z > n) & (zh == n // 4))
        def _(n=n):
            pl.semaphore_signal(ready_z, inc=1, device_id=z_devices[n], device_id_type=MESH)

        if n < 4:

            @pl.when(zh == 1)
            def _(n=n):
                pl.semaphore_signal(ready_far, inc=1, device_id=z_devices[n], device_id_type=MESH)

        @pl.when(rank > n)
        def _(n=n):
            pl.semaphore_signal(ready_y, inc=1, device_id=y_devices[n], device_id_type=MESH)

    for load in loads[1:] + base_loads:
        load.start()
    inbox[...] = jnp.zeros(inbox.shape, BF16)

    hidden_load.wait()
    everything = hfull[...].astype(F32).reshape(FRESH, D)
    for m in range(8):
        for c in range(2):
            starts = [(16 * j + 2 * m + c) * CHUNK for j in range(4)]
            columns = jnp.concatenate([everything[:, a : a + CHUNK] for a in starts], axis=1)
            hsend[m, c] = columns.reshape(STEPS, ROWS, SLICE // 2).astype(BF16)

    hbuf[y] = hsend[y]

    @pl.when(rank < 7)
    def _():
        pl.semaphore_wait(ready_y, 7 - rank)

    for k in FAR_FIRST:
        hidden_out(k).start()
    query_load.wait()
    swap = swap_matrix()
    flat = qbuf[...].astype(F32).reshape(FRESH, HEADS * HD)
    stacked = jnp.concatenate([flat[:, h * HD : (h + 1) * HD] for h in range(HEADS)], axis=0)
    qflat[...] = stacked.astype(BF16)
    qall[...] = dot(swap, stacked.astype(BF16))

    length_load.wait()
    lane = iota((ROWS, HD), 1)
    row = iota((ROWS, HD), 0)
    start = jnp.zeros((ROWS, HD), F32)
    for r in range(ROWS):
        start = jnp.where(row == r, lens[r].astype(F32), start)
    ladder = jnp.where(lane < HD // 2, lane, lane - HD // 2).astype(F32)
    freqs = jnp.exp(-math.log(1000000.0) * ladder / (HD // 2))
    for s in range(STEPS):
        angles = (start + float(s)) * freqs
        cosb[s * ROWS : (s + 1) * ROWS, :] = jnp.cos(angles)
        sine = jnp.sin(angles)
        sinb[s * ROWS : (s + 1) * ROWS, :] = jnp.where(lane < HD // 2, -sine, sine)

    key_load.wait()
    value_load.wait()
    scale = 1.0 / math.sqrt(HD)

    def attend(r, carry):
        rows = pl.ds(pl.multiple_of(r * QROWS, 8), QROWS)
        scores = dot_t(qall[rows, :].astype(BF16), kc[r]) * scale
        scores = jnp.where(iota((QROWS, CAP), 1) < lens[r], scores, -1e30)
        highest = jnp.max(scores, axis=-1, keepdims=True)
        weights = jnp.exp(scores - highest)
        total = jnp.sum(weights, axis=-1, keepdims=True)
        mixed = dot(weights.astype(BF16), vc[r])
        for s in range(STEPS):
            there = pl.ds(s * ROWS + r, HEADS, stride=FRESH)
            these = slice(s * HEADS, (s + 1) * HEADS)
            mbuf[there, :] = jnp.broadcast_to(highest[these, :], (HEADS, HD))
            lbuf[there, :] = jnp.broadcast_to(total[these, :], (HEADS, HD))
            acc[there, :] = mixed[these, :]
        return carry

    lax.fori_loop(0, EARLY, attend, 0)


    i = iota((40, 64), 0)
    tens = lax.shift_right_logical(i * 205, 11)
    pick = jnp.where(iota((40, 64), 1) == i + 6 * tens, 1.0, 0.0).astype(BF16)
    i = iota((16, 128), 0)
    column = 4 * x + jnp.where(i < 8, i, i - 6)
    wanted = (iota((16, 128), 1) == column) & ((i < 2) | ((i >= 8) & (i < 10)))
    choose = jnp.where(wanted, 1.0, 0.0).astype(BF16)
    code_load.wait()
    scale_load.wait()
    for k in range(1, 4):
        for copy in from_x(k):
            copy.wait_recv()
    for k in range(4):
        inbox[k, 0:OWNED, 0 : 2 * WIDE] = boxc[k]
        inbox[k, 0:OWNED, 2 * WIDE : 2 * WIDE + 16] = boxs[k]
    got = inbox[...].reshape(64, 2 * WIDE + 128)
    factors = dot_t(choose, jnp.concatenate([got[:, 2 * WIDE :], jnp.zeros((64, 128), BF16)], axis=0))
    body = dot(pick, got[:, : 2 * WIDE])
    for half in range(2):
        last = jnp.concatenate([factors[8 * half : 8 * half + 8, :], jnp.zeros((8, 128), F32)], axis=1)
        whole = jnp.concatenate([body[:, half * WIDE : (half + 1) * WIDE], last], axis=0)
        packed[half] = whole.astype(BF16)
    @pl.when(zh == 1)
    def _():
        for n in range(4):
            codes_out(n).start()

    @pl.when(zl < 3)
    def _():
        pl.semaphore_wait(ready_z, 3 - zl)

    for n in range(8):

        @pl.when((z != n) & (zh == n // 4))
        def _(n=n):
            codes_out(n).start()

    @pl.when(zh == 0)
    def _():
        pl.semaphore_wait(ready_far, 4)
        for n in range(4, 8):
            codes_out(n).start()

    arrived[source(z)] = packed[zh]

    lax.fori_loop(EARLY, ROWS, attend, 0)

    for load in base_loads:
        load.wait()
    i = iota((CHUNK, 96), 0)
    tens = lax.shift_right_logical(i * 205, 11)
    odd = lax.rem(tens, 2)
    within = i - 10 * tens
    pair = lax.div(tens, 2)
    pick = jnp.where(iota((CHUNK, 96), 1) == odd * 48 + pair * 10 + within, 1.0, 0.0).astype(BF16)
    i = iota((CHUNK, 256), 0)
    tens = lax.shift_right_logical(i * 205, 11)
    odd = lax.rem(tens, 2)
    within = i - 10 * tens
    pair = lax.div(tens, 2)
    spread = jnp.where(iota((CHUNK, 256), 1) == odd * 128 + pair * 16 + within, 1.0, 0.0).astype(BF16)
    for k in range(1, 8):
        hidden_in(k).wait_recv()
    for c in range(2):
        left[c] = hbuf[:, c].astype(F32).reshape(8 * FRESH, SLICE // 2).astype(BF16)
    gain_load.wait()
    for k in range(1, 8):
        codes_in(k).wait_recv()
    sides, factors = [], []
    for j in range(4):
        sides.append(arrived[2 * j : 2 * j + 2].reshape(96, WIDE))
        columns = []
        for half in range(2):
            ends = arrived[2 * j + half, 32:48, 0:128].astype(F32)
            columns.append(
                jnp.concatenate(
                    [jnp.broadcast_to(ends[8 + part : 9 + part, :], (128, 128)) for part in range(2)], axis=0
                )
            )
        factors.append(jnp.concatenate(columns, axis=1).astype(BF16))
    update = dot(pick, jnp.concatenate(sides, axis=1))
    factor = dot_t(spread, jnp.concatenate(factors, axis=0))
    for j in range(4):
        part = slice(j * WIDE, (j + 1) * WIDE)
        wbuf[core, j * CHUNK : (j + 1) * CHUNK, :] = (
            basebuf[j].astype(F32) + update[:, part] * factor[:, part]
        ).astype(BF16)
    weight_copy(core).start()

    partial = dot(left[core], wbuf[core])
    weight_copy(1 - core).wait_recv()
    partial = partial + dot(left[1 - core], wbuf[1 - core])
    pout[...] = partial.reshape(8, FRESH, WIDE)
    for k in FAR_FIRST:
        sum_out(k).start()
    pin[y] = pout[y]
    everything = qflat[...]
    shape = (HEADS, STEPS, ROWS, FRESH)
    col = iota(shape, 3)
    slot = jnp.where(col >= 2 * ROWS, 2, jnp.where(col >= ROWS, 1, 0))
    seen = (col - slot * ROWS == iota(shape, 2)) & (slot <= iota(shape, 1))
    bias = jnp.where(seen, 0.0, -1e30).astype(F32).reshape(ALLQ, FRESH)
    for k in range(1, 4):
        for copy in to_x(k):
            copy.wait_send()
    for k in FAR_FIRST:
        hidden_out(k).wait_send()
    for n in range(8):

        @pl.when(z != n)
        def _(n=n):
            codes_out(n).wait_send()

    weight_copy(core).wait_send()
    for k in range(1, 8):
        sum_in(k).wait_recv()
    projected = pin[0]
    for m in range(1, 8):
        projected = projected + pin[m]

    keys = projected[:, :HD]
    meansq = jnp.mean(keys * keys, axis=-1, keepdims=True)
    keys = keys * lax.rsqrt(meansq + 1e-06) * gain[...]
    turned = jnp.concatenate([keys[:, HD // 2 :], keys[:, : HD // 2]], axis=1)
    keys = (keys * cosb[...] + turned * sinb[...]).astype(BF16)
    values = projected[:, HD:].astype(BF16)

    scores = dot_t(everything, keys) * scale + bias
    before = mbuf[...]
    highest = jnp.maximum(before[:, :1], jnp.max(scores, axis=-1, keepdims=True))
    weights = jnp.exp(scores - highest)
    shrink = jnp.exp(before - highest)
    total = shrink * lbuf[...] + jnp.sum(weights, axis=-1, keepdims=True)
    result = (shrink * acc[...] + dot(weights.astype(BF16), values)) / total
    result = jnp.concatenate([result[h * FRESH : (h + 1) * FRESH, :] for h in range(HEADS)], axis=1)
    out_ref[...] = result.reshape(STEPS, ROWS, HEADS * HD).astype(BF16)

    for k in FAR_FIRST:
        sum_out(k).wait_send()


def per_device(hidden, queries, key_cache, value_cache, lengths, key_gain, base_weight, delta_codes, delta_scales):
    dma = pltpu.SemaphoreType.DMA
    return pl.pallas_call(
        kernel,
        out_shape=pltpu.VMEM((STEPS, ROWS, HEADS * HD), BF16),
        in_specs=[pl.BlockSpec(memory_space=pl.ANY)] * 9,
        out_specs=pl.BlockSpec(memory_space=pltpu.VMEM),
        scratch_shapes=[
            pltpu.SMEM((ROWS,), jnp.int32),
            pltpu.VMEM((1, HD), F32),
            pltpu.VMEM((4, CHUNK, WIDE), BF16),
            pltpu.VMEM((STEPS, ROWS, HEADS * HD), BF16),
            pltpu.VMEM((STEPS, ROWS, D), BF16),
            pltpu.VMEM((ROWS, CAP, HD), BF16),
            pltpu.VMEM((ROWS, CAP, HD), BF16),
            pltpu.VMEM((4, OWNED, 2 * WIDE), BF16),
            pltpu.VMEM((4, OWNED, 16), BF16),
            pltpu.VMEM((4, 16, 2 * WIDE + 128), BF16),
            pltpu.VMEM((2, 48, WIDE), BF16),
            pltpu.VMEM((8, 48, WIDE), BF16),
            pltpu.VMEM((2, SLICE // 2, WIDE), BF16),
            pltpu.VMEM((8, 2, STEPS, ROWS, SLICE // 2), BF16),
            pltpu.VMEM((8, 2, STEPS, ROWS, SLICE // 2), BF16),
            pltpu.VMEM((2, 8 * FRESH, SLICE // 2), BF16),
            pltpu.VMEM((8, FRESH, WIDE), F32),
            pltpu.VMEM((8, FRESH, WIDE), F32),
            pltpu.VMEM((ALLQ, HD), BF16),
            pltpu.VMEM((ALLQ, HD), F32),
            pltpu.VMEM((ALLQ, HD), F32),
            pltpu.VMEM((ALLQ, HD), F32),
            pltpu.VMEM((ALLQ, HD), F32),
            pltpu.VMEM((FRESH, HD), F32),
            pltpu.VMEM((FRESH, HD), F32),
            dma((8,)), dma((4,)),
            dma((4, 2)), dma((4, 2)),
            dma((8,)), dma((8,)),
            dma((8,)), dma((8,)),
            dma, dma,
            dma((8,)), dma((8,)),
            pltpu.SemaphoreType.REGULAR, pltpu.SemaphoreType.REGULAR, pltpu.SemaphoreType.REGULAR,
        ],
        compiler_params=pltpu.CompilerParams(
            collective_id=0, has_side_effects=True, vmem_limit_bytes=56 * 1024 * 1024
        ),
        name="project_and_attend",
    )(
        lengths, key_gain.reshape(1, HD), delta_codes, delta_scales, base_weight, hidden, queries, key_cache, value_cache,
    )


def solution(mesh):
    return jax.shard_map(
        per_device,
        mesh=mesh,
        in_specs=(
            P(None, "group", None),
            P(None, "group", "tp"),
            P("group", None, "tp"),
            P("group", None, "tp"),
            P("group"),
            P(),
            P(None, "tp"),
            P(("group", "tp"), None),
            P(("group", "tp"), None),
        ),
        out_specs=P(None, "group", "tp"),
        check_vma=False,
    )
```
